32 devices in a mesh: ctx: 4 (over y, core), dp: 8 (over z, x).
Axes of the slice: x: 2, y: 2, z: 4, core: 2. Of those that a mesh axis runs over, the one named last changes fastest.
Arguments:
- token_ids: int32 [8, 512], P('dp', 'ctx'), may hold values from 0 to 511
- feature_table: bfloat16 [3072, 512], replicated, may hold values from -6 to 6
- short_weight: float32 [3072, 7], replicated, may hold values from -3 to 3
- residue: float32 [1024, 16], replicated, may hold values from -0.1875 to 0.1875
- rates: float32 [16], replicated, may hold values from 0.3 to 16
- skip_gain: float32 [1024], replicated, may hold values from 0.5 to 1.5
- grad_out: bfloat16 [8, 1024, 512], P('dp', None, 'ctx'), may hold values from -0.01171875 to 0.01171875
Outputs:
- mixed: bfloat16 [8, 1024, 512], P('dp', None, 'ctx')
- grad_residue: float32 [1024, 16], replicated
- grad_rate: float32 [16], replicated
The draws below stay inside these ranges and needn't reach their ends.
All inputs are finite; a program needn't handle non-finite values.
Results may differ from the reference program's by a relative error of at most 0.0065.
Values may be sent and summed in bfloat16 or wider, within the bound.
No kernel may reach another device: no remote copies, remote signals or barrier semaphores. Data moves between devices by JAX's collectives and lax.ppermute only.
A program may use at most 64 MiB of HBM per device.

```python
import math
import jax
import jax.numpy as jnp
from jax import lax

CH = 1024
VOCAB = 512
MODES = 16
SHORT = 7
FEAT = 3072
SEQ = 512
SEQS = 8


def plant(values, stream_key, least, largest):
    longest = values.shape.index(max(values.shape))
    spots = []
    for shift in (0, 1):
        where = [jax.random.randint(jax.random.fold_in(stream_key, axis), (), 0, length) for axis, length in enumerate(values.shape)]
        where[longest] = (where[longest] + shift) % values.shape[longest]
        spots.append(tuple(where))
    return values.at[spots[0]].set(least).at[spots[1]].set(largest)


def block_scale(own_key, dims, cuts, smallest, top_value):
    def one(axis_at, blocks):
        draws = jax.random.uniform(jax.random.fold_in(jax.random.fold_in(own_key, 6), axis_at), (blocks,), jnp.float32, smallest / len(cuts), top_value / len(cuts))
        return jnp.repeat(jnp.exp(draws), dims[axis_at] // blocks).reshape((-1,) + (1,) * (len(dims) - axis_at - 1))

    factor_of = one(*cuts[0])
    for cut in cuts[1:]:
        factor_of = factor_of * one(*cut)
    return factor_of


def gaussian(rng, shape, scale, limit, pieces=(), held_as=jnp.bfloat16):
    level = block_scale(rng, shape, pieces, -0.22, 0.18) if pieces else 1.0
    values = jax.random.normal(rng, shape, jnp.float32) * scale * level
    return jnp.minimum(jnp.maximum(values, -limit), limit).astype(held_as)


def setup_inputs(seed: int = 0) -> dict:
    keys = jax.random.split(jax.random.key(seed), 8)
    return {
        "token_ids": plant(jax.random.randint(keys[0], (SEQS, SEQ), 0, VOCAB), jax.random.fold_in(keys[0], 1), 0, VOCAB - 1).astype(jnp.int32),
        "feature_table": gaussian(keys[1], (FEAT, VOCAB), 1.0, 6.0),
        "short_weight": gaussian(keys[2], (FEAT, SHORT), 0.5, 3.0, (), jnp.float32),
        "residue": gaussian(keys[3], (CH, MODES), (MODES * SEQ // 8) ** -0.5, 0.1875, (), jnp.float32),
        "rates": jnp.clip(jnp.exp(jax.random.uniform(keys[4], (MODES,), jnp.float32, math.log(0.3), math.log(16.0))), 0.3, 16.0),
        "skip_gain": jnp.clip(1.0 + 0.1 * jax.random.normal(keys[5], (CH,), jnp.float32), 0.5, 1.5),
        "grad_out": gaussian(keys[6], (SEQS, CH, SEQ), (1.0 / (8 * (SEQS * SEQ) ** 0.5)), 0.01171875, ((0, 8), (2, 4))),
    }


def reference(token_ids, feature_table, short_weight, residue, rates, skip_gain, grad_out):
    steps_i = jnp.arange(SEQ, dtype=jnp.int32)
    steps_f = steps_i.astype(jnp.float32)
    period = 2 * MODES + 2
    mode_number = jnp.arange(MODES, dtype=jnp.int32)[:, None] + 1
    angles = (mode_number * steps_i[None, :] % period).astype(jnp.float32) * (2.0 * math.pi / period)
    oscillation = jnp.cos(angles)

    def make_taps(weights, decays):
        powers = jnp.exp(-decays[:, None] * steps_f[None, :] / SEQ) * oscillation
        return jnp.dot(weights, powers, precision=lax.Precision.HIGHEST)

    def circular_conv(filt, signal):
        spectrum = jnp.fft.rfft(signal, SEQ) * jnp.fft.rfft(filt, SEQ)
        return jnp.fft.irfft(spectrum, SEQ)

    def one_sequence(pair):
        ids_row, cotangent = pair
        features = jnp.take(feature_table, ids_row, axis=1).astype(jnp.float32)
        padded = jnp.concatenate([features[:, SEQ - (SHORT - 1):], features], axis=1)
        mixer = jnp.zeros((FEAT, SEQ), jnp.float32)
        for offset in range(SHORT):
            mixer = mixer + short_weight[:, offset:offset + 1] * padded[:, offset:offset + SEQ]
        queries = mixer[:CH]
        keys_part = mixer[CH:2 * CH]
        values_part = mixer[2 * CH:]
        gated = lax.optimization_barrier((keys_part * values_part).astype(jnp.bfloat16)).astype(jnp.float32)
        conv, pullback = jax.vjp(lambda weights, decays: circular_conv(make_taps(weights, decays), gated), residue, rates)
        mixed = (queries * (conv + skip_gain[:, None] * gated)).astype(jnp.bfloat16)
        dconv = queries * cotangent.astype(jnp.float32)
        grad_weights, grad_decays = pullback(dconv)
        return (mixed, grad_weights, grad_decays)
    mixed, grad_weights, grad_decays = lax.map(one_sequence, (token_ids, grad_out))
    return (mixed, lax.optimization_barrier(jnp.sum(grad_weights, axis=0)), lax.optimization_barrier(jnp.sum(grad_decays, axis=0)))
```

```python
import functools
import math

import jax
import jax.numpy as jnp
import numpy as np
from jax import lax
from jax.experimental import pallas as pl
from jax.experimental.pallas import tpu as pltpu
from jax.sharding import PartitionSpec as P

F32 = jnp.float32
BF16 = jnp.bfloat16
GROUP = 256
HALO = 8
LANES = 128


def xor_permute(block, axis, mask):
    return lax.ppermute(block, axis, [(i, i ^ mask) for i in range(lax.axis_size(axis))])


def masks_of(size):
    return [1 << bit for bit in range(size.bit_length() - 1)]


def halves(table):
    upper = table.astype(BF16)
    return upper, (table - upper.astype(F32)).astype(BF16)


def dot(left, right):
    return jnp.dot(left, right, preferred_element_type=F32)


def dft_tables(block_len):
    period = 2 * block_len
    column = np.arange(block_len)[:, None]
    sample = np.arange(period)[None, :]
    angle = (column * sample % period) * (2.0 * math.pi / period)
    parity = 1.0 - 2.0 * (sample % 2)
    imag = np.where(column == 0, parity, -np.sin(angle))
    forward = np.concatenate([np.cos(angle), imag], axis=0)
    weight = np.where(np.arange(period) % block_len == 0, 1.0, 2.0) / period
    inverse = (forward[:, :block_len] * weight[:, None]).T
    return forward, inverse, weight


def np_halves(table):
    upper = table.astype(np.float32).astype(jnp.bfloat16)
    lower = (table - upper.astype(np.float64)).astype(np.float32).astype(jnp.bfloat16)
    return upper, lower


def mode_constants(block_len, seq_len, modes):
    near = np.arange(2 * block_len)
    near = np.where(near < block_len, near, seq_len - 2 * block_len + near)
    far = seq_len - block_len - np.arange(seq_len - block_len)
    here = np.arange(block_len)
    delay = np.concatenate([near, far, here])[:, None]
    period = 2 * modes + 2
    angle = (delay * (np.arange(modes)[None, :] + 1) % period) * (2.0 * math.pi / period)
    ratio = delay / seq_len
    parts = [np.cos(angle), np.sin(angle), -ratio * np.cos(angle), -ratio * np.sin(angle)]
    wave = np.concatenate(parts, axis=1)
    wave = np.pad(wave, ((0, 0), (0, LANES - wave.shape[1])))
    return wave.astype(np.float32), (-ratio).astype(np.float32)


def tables_kernel(modes, block_len, seq_len, rates_ref, wave_ref, ratio_ref, fwd_ref, weight_ref, res_ref, grad_ref,
                  far_ref, here_ref, here_t_ref, near_ref, filt_ref, grad_t_ref, rate_row):
    rate_row[...] = jnp.zeros_like(rate_row)
    rate_row[:, :modes] = rates_ref[...]
    rates = rate_row[...]
    for shift in (modes, 2 * modes):
        rates = rates + pltpu.roll(rates, shift, 1)
    table = jnp.exp(ratio_ref[...] * rates) * wave_ref[...]
    near = table[: 2 * block_len]
    far = table[2 * block_len : 2 * block_len + seq_len - block_len]
    here = table[2 * block_len + seq_len - block_len :]
    used = 4 * modes
    far_t = halves(far.T[:used])
    far_ref[...] = jnp.concatenate(far_t, axis=0)
    here_t = halves(here.T[:used])
    here_ref[...] = jnp.concatenate(here_t, axis=0)
    here_t_ref[...] = here
    near_hi, near_lo = halves(near)
    fwd = fwd_ref[...]
    fwd_hi = fwd[: 2 * block_len]
    fwd_lo = fwd[2 * block_len :]
    spec = dot(fwd_hi, near_hi) + dot(fwd_hi, near_lo) + dot(fwd_lo, near_hi)
    spec_t = (spec * weight_ref[...]).T
    grad_rows = jnp.concatenate([spec_t[:modes], spec_t[2 * modes : 3 * modes]], axis=0)
    near_ref[...] = jnp.concatenate(halves(grad_rows), axis=0)
    spec_hi, spec_lo = halves(spec[:, :modes])
    res_hi, res_lo = halves(res_ref[...])
    filt_ref[...] = dot(spec_hi, res_hi) + dot(spec_hi, res_lo) + dot(spec_lo, res_hi)
    grad_t_ref[...] = grad_ref[...].astype(F32).T


def main_kernel(modes, blocks, block_len, taps, channels, ids_ref, table_ref, short_ref, res_ref, fwd_ref, far_ref,
                here_ref, near_ref, grad_t_ref, part_ref, query_ref, gated_ref, spec_ref, state_ref,
                onehot, feat_k, feat_v, feat_q):
    seq_len = blocks * block_len
    vocab = table_ref.shape[1]
    own = lax.axis_index("ctx")
    for place in range(blocks):
        source = lax.rem(own + 1 + place, blocks)
        row = ids_ref[pl.ds(source ^ own, 1), :]
        column = jnp.broadcast_to(row, (block_len, block_len)).T
        lane = lax.broadcasted_iota(jnp.int32, (block_len, block_len), 1)
        for piece in range(vocab // block_len):
            match = column == lane + piece * block_len
            onehot[pl.ds(place * block_len, block_len), pl.ds(piece * block_len, block_len)] = jnp.where(
                match, 1.0, 0.0
            ).astype(BF16)
    hot = onehot[...]
    first = HALO - (taps - 1)
    body = seq_len - block_len
    period = 2 * block_len
    rate = jnp.zeros((modes, 1), F32)
    groups = channels // GROUP

    def gather(rows, hot):
        block = table_ref[pl.ds(rows, GROUP), :]
        return lax.dot_general(hot, block, (((1,), (1,)), ((), ())), preferred_element_type=F32)

    def short_conv(feat, rows, length, side):
        total = None
        for tap in range(taps):
            weight = short_ref[tap : tap + 1, pl.ds(rows + side * LANES, LANES)]
            term = weight * feat[side, pl.ds(first + tap, length), :]
            total = term if total is None else total + term
        return total

    def one_group(base, rate):
        for feat, offset in ((feat_k, channels), (feat_v, 2 * channels)):
            values = gather(offset + base, hot)
            for side in range(GROUP // LANES):
                cols = values[:, side * LANES : (side + 1) * LANES]
                feat[side, HALO:, :] = cols
                feat[side, :HALO, :] = cols[seq_len - HALO :]
        values = gather(base, hot[body - HALO if blocks > 1 else 0 :])
        for side in range(GROUP // LANES):
            feat_q[side, :, :] = values[:, side * LANES : (side + 1) * LANES]
        gated = []
        query = []
        for side in range(GROUP // LANES):
            keys = short_conv(feat_k, channels + base, seq_len, side)
            vals = short_conv(feat_v, 2 * channels + base, seq_len, side)
            gated.append((keys * vals).astype(BF16))
            query.append(short_conv(feat_q, base, block_len, side))
        gated = jnp.concatenate(gated, axis=1)
        query = jnp.concatenate(query, axis=1)
        span = pl.ds(base, GROUP)
        query_ref[:, span] = query
        gated_own = gated[body:]
        gated_ref[:, span] = gated_own
        dconv = query * grad_t_ref[:, span]
        dconv_both = jnp.concatenate(halves(dconv), axis=0)
        spec = dot(fwd_ref[...], gated_own)
        spec = spec[:period] + spec[period:]
        spec_ref[:, span] = spec
        left = jnp.concatenate([fwd_ref[...], here_ref[...]], axis=0)
        dspec = dot(jnp.concatenate([left, left], axis=1), dconv_both)
        dstate = dspec[2 * period :]
        dspec = dspec[:period] + dspec[period : 2 * period]
        dstate = dstate[: 4 * modes] + dstate[4 * modes :]
        state = dot(far_ref[...], gated[:body])
        state = state[: 4 * modes] + state[4 * modes :]
        left_re, left_im = spec[:block_len], spec[block_len:]
        right_re, right_im = dspec[:block_len], dspec[block_len:]
        leading = lax.broadcasted_iota(jnp.int32, (block_len, GROUP), 0) == 0
        rere, imim = left_re * right_re, left_im * right_im
        cross_re = jnp.where(leading, rere, rere + imim)
        cross_im = jnp.where(leading, imim, left_re * right_im - left_im * right_re)
        cross = jnp.concatenate([cross_re, cross_im], axis=0)
        cross_hi, cross_lo = halves(cross)
        near = near_ref[...]
        terms = dot(near, cross_hi) + dot(near, cross_lo)
        terms = terms[: 2 * modes] + terms[2 * modes :]
        sc, ss, sc1, ss1 = (state[i * modes : (i + 1) * modes] for i in range(4))
        dc, ds, dc1, ds1 = (dstate[i * modes : (i + 1) * modes] for i in range(4))
        grad = terms[:modes] + dc * sc - ds * ss
        slope = terms[modes:] + dc1 * sc + dc * sc1 - ds1 * ss - ds * ss1
        res = res_ref[:, span]
        state_ref[:modes, span] = res * sc
        state_ref[modes:, span] = -(res * ss)
        for side in range(GROUP // LANES):
            at = (base + side * LANES) // LANES * modes
            part_ref[pl.ds(at, modes), :] = grad[:, side * LANES : (side + 1) * LANES]
        return rate + jnp.sum(res * slope, axis=1, keepdims=True)

    if blocks <= 4:
        for group in range(groups):
            rate = one_group(group * GROUP, rate)
    else:
        rate = lax.fori_loop(0, groups, lambda g, r: one_group(pl.multiple_of(g * GROUP, GROUP), r), rate)
    wide = jnp.broadcast_to(rate, (modes, LANES))
    square = jnp.concatenate([wide, jnp.zeros((LANES - modes, LANES), F32)], axis=0).T
    part_ref[pl.ds(channels // LANES * modes, 8), :] = square[:8]


def mixed_kernel(modes, block_len, query_ref, gated_ref, spec_ref, filt_ref, state_ref, here_t_ref, inv_ref, skip_ref,
                 out_ref):
    channels = query_ref.shape[1]
    period = 2 * block_len
    leading = lax.broadcasted_iota(jnp.int32, (block_len, GROUP), 0) == 0
    inv = inv_ref[...]
    inv_hi, inv_lo = inv[:block_len], inv[block_len:]
    here_hi, here_lo = halves(here_t_ref[:, : 2 * modes])
    for base in range(0, channels, GROUP):
        span = pl.ds(base, GROUP)
        left_re, left_im = filt_ref[:block_len, span], filt_ref[block_len:, span]
        right_re, right_im = spec_ref[:block_len, span], spec_ref[block_len:, span]
        rere, imim = left_re * right_re, left_im * right_im
        out_re = jnp.where(leading, rere, rere - imim)
        out_im = jnp.where(leading, imim, left_re * right_im + left_im * right_re)
        prod_hi, prod_lo = halves(jnp.concatenate([out_re, out_im], axis=0))
        conv = dot(inv_hi, prod_hi) + dot(inv_hi, prod_lo) + dot(inv_lo, prod_hi)
        state_hi, state_lo = halves(state_ref[:, span])
        conv = conv + dot(here_hi, state_hi) + dot(here_hi, state_lo) + dot(here_lo, state_hi)
        mixed = query_ref[:, span] * (conv + skip_ref[:, span] * gated_ref[:, span].astype(F32))
        out_ref[pl.ds(base, GROUP), :] = mixed.T.astype(BF16)


def vmem_call(kernel, outs, scratch, args, flops, moved):
    return pl.pallas_call(
        kernel,
        out_shape=[jax.ShapeDtypeStruct(shape, dtype) for shape, dtype in outs],
        in_specs=[pl.BlockSpec(memory_space=pltpu.VMEM)] * len(args),
        out_specs=[pl.BlockSpec(memory_space=pltpu.VMEM)] * len(outs),
        scratch_shapes=scratch,
        compiler_params=pltpu.CompilerParams(vmem_limit_bytes=40 * 1024 * 1024),
        cost_estimate=pl.CostEstimate(flops=flops, bytes_accessed=moved, transcendentals=0),
    )(*args)


def per_device(token_ids, feature_table, short_weight, residue, rates, skip_gain, grad_out):
    block_len = token_ids.shape[1]
    blocks = lax.axis_size("ctx")
    seq_len = block_len * blocks
    channels, modes = residue.shape
    taps = short_weight.shape[1]
    vocab = feature_table.shape[1]
    period = 2 * block_len
    forward, inverse, weight = dft_tables(block_len)
    fwd_hi, fwd_lo = np_halves(forward)
    fwd_all = np.concatenate([fwd_hi, fwd_lo], axis=0)
    inv_all = np.concatenate(np_halves(inverse), axis=0)
    wave, ratio = mode_constants(block_len, seq_len, modes)
    res_t = residue.T

    ids = token_ids
    for mask in masks_of(blocks):
        ids = jnp.concatenate([ids, xor_permute(ids, "ctx", mask)], axis=0)

    far, here, here_t, near, filt, grad_t = vmem_call(
        functools.partial(tables_kernel, modes, block_len, seq_len),
        [
            ((8 * modes, seq_len - block_len), BF16),
            ((8 * modes, block_len), BF16),
            ((block_len, LANES), F32),
            ((4 * modes, period), BF16),
            ((period, channels), F32),
            ((block_len, channels), F32),
        ],
        [pltpu.VMEM((1, LANES), F32)],
        [
            rates[None],
            jnp.asarray(wave),
            jnp.asarray(ratio),
            jnp.asarray(fwd_all),
            jnp.asarray(weight[:, None].astype(np.float32)),
            res_t,
            grad_out[0],
        ],
        100_000_000,
        2_000_000,
    )
    part, query, gated, spec, state = vmem_call(
        functools.partial(main_kernel, modes, blocks, block_len, taps, channels),
        [
            ((channels // LANES * modes + 8, LANES), F32),
            ((block_len, channels), F32),
            ((block_len, channels), BF16),
            ((period, channels), F32),
            ((2 * modes, channels), F32),
        ],
        [
            pltpu.VMEM((seq_len, vocab), BF16),
            pltpu.VMEM((GROUP // LANES, seq_len + HALO, LANES), F32),
            pltpu.VMEM((GROUP // LANES, seq_len + HALO, LANES), F32),
            pltpu.VMEM((GROUP // LANES, block_len + HALO, LANES), F32),
        ],
        [
            ids,
            feature_table,
            short_weight.T,
            res_t,
            jnp.asarray(fwd_all[:, :block_len]),
            far,
            here,
            near,
            grad_t,
        ],
        2 * seq_len * vocab * 3 * channels,
        6_000_000,
    )
    (mixed,) = vmem_call(
        functools.partial(mixed_kernel, modes, block_len),
        [((channels, block_len), BF16)],
        [],
        [query, gated, spec, filt, state, here_t, jnp.asarray(inv_all), skip_gain[None]],
        300_000_000,
        3_000_000,
    )
    for axis in ("ctx", "dp"):
        for mask in masks_of(lax.axis_size(axis)):
            part = part + xor_permute(part, axis, mask)
    rows = channels // LANES * modes
    grad_res = part[:rows].reshape(channels // LANES, modes, LANES).transpose(0, 2, 1).reshape(channels, modes)
    return (mixed[None], grad_res, part[rows, :modes])


def solution(mesh):
    return jax.shard_map(
        per_device,
        mesh=mesh,
        in_specs=(P("dp", "ctx"), P(), P(), P(), P(), P(), P("dp", None, "ctx")),
        out_specs=(P("dp", None, "ctx"), P(), P()),
        check_vma=False,
    )
```

```python
import functools
import math

import jax
import jax.numpy as jnp
import numpy as np
from jax import lax
from jax.experimental import pallas as pl
from jax.experimental.pallas import tpu as pltpu
from jax.sharding import PartitionSpec as P

F32 = jnp.float32
BF16 = jnp.bfloat16
GROUP = 256
HALO = 8
LANES = 128


def xor_permute(block, axis, mask):
    size = math.prod(lax.axis_size(name) for name in axis)
    return lax.ppermute(block, axis, [(i, i ^ mask) for i in range(size)])


def masks_of(size):
    return [1 << bit for bit in range(size.bit_length() - 1)]


def halves(table):
    upper = table.astype(BF16)
    return upper, (table - upper.astype(F32)).astype(BF16)


def dot(left, right):
    return jnp.dot(left, right, preferred_element_type=F32)


def dft_tables(block_len):
    period = 2 * block_len
    column = np.arange(block_len)[:, None]
    sample = np.arange(period)[None, :]
    angle = (column * sample % period) * (2.0 * math.pi / period)
    parity = 1.0 - 2.0 * (sample % 2)
    imag = np.where(column == 0, parity, -np.sin(angle))
    forward = np.concatenate([np.cos(angle), imag], axis=0)
    weight = np.where(np.arange(period) % block_len == 0, 1.0, 2.0) / period
    inverse = (forward[:, :block_len] * weight[:, None]).T
    return forward, inverse


def mode_constants(block_len, seq_len, modes):
    near = np.arange(2 * block_len)
    near = np.where(near < block_len, near, seq_len - 2 * block_len + near)
    far = seq_len - block_len - np.arange(seq_len - block_len)
    here = np.arange(block_len)
    delay = np.concatenate([near, far, here])[:, None]
    period = 2 * modes + 2
    angle = (delay * (np.arange(modes)[None, :] + 1) % period) * (2.0 * math.pi / period)
    ratio = delay / seq_len
    parts = [np.cos(angle), np.sin(angle), -ratio * np.cos(angle), -ratio * np.sin(angle)]
    wave = np.concatenate(parts, axis=1)
    return np.pad(wave, ((0, 0), (0, LANES - wave.shape[1]))).astype(np.float32)


def tables_kernel(modes, block_len, seq_len, *refs):
    sources, outs, scratch = refs[:10], refs[10:23], refs[23:]
    (ids_out, table_out, short_out, res_out, skip_out, fwd_out, inv_out, far_ref, here_ref, here_t_ref, near_ref,
     filt_ref, grad_t_ref) = outs
    few, rate_row, wave, fwd, inv, grad, copied = scratch
    rate_row[...] = jnp.zeros_like(rate_row)
    targets = [wave, few, fwd, res_out, grad, inv, ids_out, short_out, skip_out, table_out]
    copies = [
        pltpu.make_async_copy(source, target, copied.at[i])
        for i, (source, target) in enumerate(zip(sources, targets, strict=True))
    ]
    for copy in copies:
        copy.start()
    period = 2 * block_len
    body = seq_len - block_len
    copies[0].wait()
    copies[1].wait()
    rate_row[:, :modes] = few[...]
    rates = rate_row[...]
    for shift in (modes, 2 * modes):
        rates = rates + pltpu.roll(rates, shift, 1)

    def table_of(start, length, delay):
        place = lax.broadcasted_iota(jnp.int32, (length, LANES), 0)
        return jnp.exp(delay(place).astype(F32) * (-1.0 / seq_len) * rates) * wave[pl.ds(start, length), :]

    near = table_of(0, period, lambda n: jnp.where(n < block_len, n, n + (seq_len - period)))
    far = table_of(period, body, lambda n: body - n)
    here = table_of(period + body, block_len, lambda n: n)
    used = 4 * modes
    far_ref[...] = jnp.concatenate(halves(far.T[:used]), axis=0)
    here_ref[...] = jnp.concatenate(halves(here.T[:used]), axis=0)
    here_t_ref[...] = here
    near_hi, near_lo = halves(near)
    copies[2].wait()
    fwd_hi, fwd_lo = halves(fwd[...])
    fwd_out[:period, :] = fwd_hi[:, :block_len]
    fwd_out[period:, :] = fwd_lo[:, :block_len]
    spec = dot(fwd_hi, near_hi) + dot(fwd_hi, near_lo) + dot(fwd_lo, near_hi)
    place = lax.broadcasted_iota(jnp.int32, (period, LANES), 0)
    weight = jnp.where(lax.rem(place, block_len) == 0, 1.0 / period, 2.0 / period)
    spec_t = (spec * weight).T
    grad_rows = jnp.concatenate([spec_t[:modes], spec_t[2 * modes : 3 * modes]], axis=0)
    near_ref[...] = jnp.concatenate(halves(grad_rows), axis=0)
    copies[3].wait()
    spec_hi, spec_lo = halves(spec[:, :modes])
    res_hi, res_lo = halves(res_out[...])
    filt_ref[...] = dot(spec_hi, res_hi) + dot(spec_hi, res_lo) + dot(spec_lo, res_hi)
    copies[4].wait()
    grad_t_ref[...] = grad[...].astype(F32).T
    copies[5].wait()
    inv_out[...] = jnp.concatenate(halves(inv[...]), axis=0)
    for copy in copies[6:]:
        copy.wait()


def main_kernel(modes, blocks, block_len, taps, channels, ids_ref, table_ref, short_ref, res_ref, fwd_ref, far_ref,
                here_ref, near_ref, grad_t_ref, part_ref, rate_ref, query_ref, gated_ref, spec_ref, state_ref,
                onehot, feat_k, feat_v, feat_q):
    seq_len = blocks * block_len
    vocab = table_ref.shape[1]
    own = lax.axis_index("ctx")
    bits = blocks.bit_length() - 1
    for place in range(blocks):
        source = lax.rem(own + 1 + place, blocks)
        place_of = source ^ own
        flags = [(place_of >> bit) & 1 for bit in range(bits)]
        slot = sum(flag << (bits - 1 - bit) for bit, flag in enumerate(flags) if bit > 0)
        slot = slot | (functools.reduce(lambda a, b: a ^ b, flags) << (bits - 1))
        row = ids_ref[pl.ds(slot, 1), :]
        column = jnp.broadcast_to(row, (block_len, block_len)).T
        lane = lax.broadcasted_iota(jnp.int32, (block_len, block_len), 1)
        for piece in range(vocab // block_len):
            match = column == lane + piece * block_len
            onehot[pl.ds(place * block_len, block_len), pl.ds(piece * block_len, block_len)] = jnp.where(
                match, 1.0, 0.0
            ).astype(BF16)
    hot = onehot[...]
    first = HALO - (taps - 1)
    body = seq_len - block_len
    period = 2 * block_len
    rate = jnp.zeros((modes, 1), F32)
    groups = channels // GROUP

    def gather(rows, hot):
        block = table_ref[pl.ds(rows, GROUP), :]
        return lax.dot_general(hot, block, (((1,), (1,)), ((), ())), preferred_element_type=F32)

    def short_conv(feat, rows, length, side):
        total = None
        for tap in range(taps):
            weight = short_ref[tap : tap + 1, pl.ds(rows + side * LANES, LANES)]
            term = weight * feat[side, pl.ds(first + tap, length), :]
            total = term if total is None else total + term
        return total

    def one_group(base, rate):
        for feat, offset in ((feat_k, channels), (feat_v, 2 * channels)):
            values = gather(offset + base, hot)
            for side in range(GROUP // LANES):
                cols = values[:, side * LANES : (side + 1) * LANES]
                feat[side, HALO:, :] = cols
                feat[side, :HALO, :] = cols[seq_len - HALO :]
        values = gather(base, hot[body - HALO if blocks > 1 else 0 :])
        for side in range(GROUP // LANES):
            feat_q[side, :, :] = values[:, side * LANES : (side + 1) * LANES]
        gated = []
        query = []
        for side in range(GROUP // LANES):
            keys = short_conv(feat_k, channels + base, seq_len, side)
            vals = short_conv(feat_v, 2 * channels + base, seq_len, side)
            gated.append((keys * vals).astype(BF16))
            query.append(short_conv(feat_q, base, block_len, side))
        gated = jnp.concatenate(gated, axis=1)
        query = jnp.concatenate(query, axis=1)
        span = pl.ds(base, GROUP)
        query_ref[:, span] = query
        gated_own = gated[body:]
        gated_ref[:, span] = gated_own
        dconv = query * grad_t_ref[:, span]
        dconv_both = jnp.concatenate(halves(dconv), axis=0)
        spec = dot(fwd_ref[...], gated_own)
        spec = spec[:period] + spec[period:]
        spec_ref[:, span] = spec
        left = jnp.concatenate([fwd_ref[...], here_ref[...]], axis=0)
        dspec = dot(jnp.concatenate([left, left], axis=1), dconv_both)
        dstate = dspec[2 * period :]
        dspec = dspec[:period] + dspec[period : 2 * period]
        dstate = dstate[: 4 * modes] + dstate[4 * modes :]
        state = dot(far_ref[...], gated[:body])
        state = state[: 4 * modes] + state[4 * modes :]
        left_re, left_im = spec[:block_len], spec[block_len:]
        right_re, right_im = dspec[:block_len], dspec[block_len:]
        leading = lax.broadcasted_iota(jnp.int32, (block_len, GROUP), 0) == 0
        rere, imim = left_re * right_re, left_im * right_im
        cross_re = jnp.where(leading, rere, rere + imim)
        cross_im = jnp.where(leading, imim, left_re * right_im - left_im * right_re)
        cross = jnp.concatenate([cross_re, cross_im], axis=0)
        cross_hi, cross_lo = halves(cross)
        near = near_ref[...]
        terms = dot(near, cross_hi) + dot(near, cross_lo)
        terms = terms[: 2 * modes] + terms[2 * modes :]
        sc, ss, sc1, ss1 = (state[i * modes : (i + 1) * modes] for i in range(4))
        dc, ds, dc1, ds1 = (dstate[i * modes : (i + 1) * modes] for i in range(4))
        grad = terms[:modes] + dc * sc - ds * ss
        slope = terms[modes:] + dc1 * sc + dc * sc1 - ds1 * ss - ds * ss1
        res = res_ref[:, span]
        state_ref[:modes, span] = res * sc
        state_ref[modes:, span] = -(res * ss)
        for side in range(GROUP // LANES):
            at = (base + side * LANES) // LANES * modes
            part_ref[pl.ds(at, modes), :] = grad[:, side * LANES : (side + 1) * LANES]
        return rate + jnp.sum(res * slope, axis=1, keepdims=True)

    if blocks <= 4:
        for group in range(groups):
            rate = one_group(group * GROUP, rate)
    else:
        rate = lax.fori_loop(0, groups, lambda g, r: one_group(pl.multiple_of(g * GROUP, GROUP), r), rate)
    wide = jnp.broadcast_to(rate, (modes, LANES))
    square = jnp.concatenate([wide, jnp.zeros((LANES - modes, LANES), F32)], axis=0).T
    rate_ref[...] = square[:8]


def mixed_kernel(modes, block_len, query_ref, gated_ref, spec_ref, filt_ref, state_ref, here_t_ref, inv_ref, skip_ref,
                 out_ref):
    channels = query_ref.shape[1]
    period = 2 * block_len
    leading = lax.broadcasted_iota(jnp.int32, (block_len, GROUP), 0) == 0
    inv = inv_ref[...]
    inv_hi, inv_lo = inv[:block_len], inv[block_len:]
    here_hi, here_lo = halves(here_t_ref[:, : 2 * modes])
    for base in range(0, channels, GROUP):
        span = pl.ds(base, GROUP)
        left_re, left_im = filt_ref[:block_len, span], filt_ref[block_len:, span]
        right_re, right_im = spec_ref[:block_len, span], spec_ref[block_len:, span]
        rere, imim = left_re * right_re, left_im * right_im
        out_re = jnp.where(leading, rere, rere - imim)
        out_im = jnp.where(leading, imim, left_re * right_im + left_im * right_re)
        prod_hi, prod_lo = halves(jnp.concatenate([out_re, out_im], axis=0))
        conv = dot(inv_hi, prod_hi) + dot(inv_hi, prod_lo) + dot(inv_lo, prod_hi)
        state_hi, state_lo = halves(state_ref[:, span])
        conv = conv + dot(here_hi, state_hi) + dot(here_hi, state_lo) + dot(here_lo, state_hi)
        mixed = query_ref[:, span] * (conv + skip_ref[:, span] * gated_ref[:, span].astype(F32))
        out_ref[pl.ds(base, GROUP), :] = mixed.T.astype(BF16)


def call(kernel, outs, scratch, args, cost, space=pltpu.VMEM):
    return pl.pallas_call(
        kernel,
        out_shape=[jax.ShapeDtypeStruct(shape, dtype) for shape, dtype in outs],
        in_specs=[pl.BlockSpec(memory_space=space)] * len(args),
        out_specs=[pl.BlockSpec(memory_space=pltpu.VMEM)] * len(outs),
        scratch_shapes=scratch,
        compiler_params=pltpu.CompilerParams(vmem_limit_bytes=40 * 1024 * 1024),
        cost_estimate=pl.CostEstimate(flops=cost[0], bytes_accessed=cost[1], transcendentals=0),
    )(*args)


def sum_kernel(modes, part_ref, moved_ref, grad_ref, rate_ref):
    tiles = grad_ref.shape[1] // LANES
    for tile in range(tiles):
        rows = pl.ds(tile * modes, modes)
        grad_ref[:, tile * LANES : (tile + 1) * LANES] = part_ref[rows, :] + moved_ref[rows, :].astype(F32)
    rest = moved_ref[tiles * modes : tiles * modes + 16, :].astype(F32)
    rate = part_ref[tiles * modes : tiles * modes + 1, :] + rest[:1] + rest[1:2]
    rate_ref[...] = rate[:, :modes]


def rounded(value):
    return lax.reduce_precision(value, 8, 7)


def per_device(token_ids, feature_table, short_weight, residue, rates, skip_gain, grad_out):
    block_len = token_ids.shape[1]
    blocks = lax.axis_size("ctx")
    seq_len = block_len * blocks
    channels, modes = residue.shape
    taps = short_weight.shape[1]
    vocab = feature_table.shape[1]
    period = 2 * block_len
    forward, inverse = dft_tables(block_len)
    wave = mode_constants(block_len, seq_len, modes)
    rows = channels // LANES * modes

    masks = [mask | 1 for mask in masks_of(blocks)[:0:-1]] + [1]
    first = xor_permute(token_ids, ("ctx",), masks[0])
    sources = [
        jnp.asarray(wave),
        rates[None],
        jnp.asarray(forward.astype(np.float32)),
        residue.T,
        grad_out[0],
        jnp.asarray(inverse.astype(np.float32)),
        token_ids,
        short_weight.T,
        skip_gain[None],
        feature_table,
    ]
    ids, table, short, res, skip, fwd, inv, far, here, here_t, near, filt, grad_t = call(
        functools.partial(tables_kernel, modes, block_len, seq_len),
        [
            ((1, block_len), jnp.int32),
            (feature_table.shape, BF16),
            (short_weight.shape[::-1], F32),
            ((modes, channels), F32),
            ((1, channels), F32),
            ((2 * period, block_len), BF16),
            ((2 * block_len, period), BF16),
            ((8 * modes, seq_len - block_len), BF16),
            ((8 * modes, block_len), BF16),
            ((block_len, LANES), F32),
            ((4 * modes, period), BF16),
            ((period, channels), F32),
            ((block_len, channels), F32),
        ],
        [
            pltpu.VMEM((1, modes), F32),
            pltpu.VMEM((1, LANES), F32),
            pltpu.VMEM(wave.shape, F32),
            pltpu.VMEM(forward.shape, F32),
            pltpu.VMEM(inverse.shape, F32),
            pltpu.VMEM(grad_out.shape[1:], BF16),
            pltpu.SemaphoreType.DMA((len(sources),)),
        ],
        [pltpu.with_memory_space_constraint(source, pltpu.HBM) for source in sources],
        (200_000_000, 5_000_000),
        pltpu.HBM,
    )
    ids = jnp.concatenate([ids, first], axis=0)
    for mask in masks[1:]:
        ids = jnp.concatenate([ids, xor_permute(ids, ("ctx",), mask)], axis=0)
    part, rate, query, gated, spec, state = call(
        functools.partial(main_kernel, modes, blocks, block_len, taps, channels),
        [
            ((rows, LANES), F32),
            ((8, LANES), F32),
            ((block_len, channels), F32),
            ((block_len, channels), BF16),
            ((period, channels), F32),
            ((2 * modes, channels), F32),
        ],
        [
            pltpu.VMEM((seq_len, vocab), BF16),
            pltpu.VMEM((GROUP // LANES, seq_len + HALO, LANES), F32),
            pltpu.VMEM((GROUP // LANES, seq_len + HALO, LANES), F32),
            pltpu.VMEM((GROUP // LANES, block_len + HALO, LANES), F32),
        ],
        [ids, table, short, res, fwd, far, here, near, grad_t],
        (2 * seq_len * vocab * 3 * channels, 6_000_000),
    )
    (mixed,) = call(
        functools.partial(mixed_kernel, modes, block_len),
        [((channels, block_len), BF16)],
        [],
        [query, gated, spec, filt, state, here_t, inv, skip],
        (300_000_000, 3_000_000),
    )
    replicas = lax.axis_size("dp")
    core = replicas
    hops = [core] + [core | mask for mask in masks_of(blocks * replicas) if mask != core]
    filler = jnp.zeros((14, LANES), BF16)
    for mask in hops:
        part = rounded(part)
        upper = rounded(rate[:1])
        lower = rounded(rate[:1] - upper)
        sent = jnp.concatenate([part.astype(BF16), upper.astype(BF16), lower.astype(BF16), filler], axis=0)
        moved = xor_permute(sent, ("ctx", "dp"), mask)
        if mask != hops[-1]:
            part = part + moved[:rows].astype(F32)
            rate = upper + lower + (moved[rows : rows + 1].astype(F32) + moved[rows + 1 : rows + 2].astype(F32))
    kept = jnp.concatenate([part, upper + lower], axis=0)
    grad, rate = call(
        functools.partial(sum_kernel, modes),
        [((modes, channels), F32), ((1, modes), F32)],
        [],
        [kept, moved],
        (0, 200_000),
    )
    return (mixed[None], grad.T, rate[0])


def solution(mesh):
    return jax.shard_map(
        per_device,
        mesh=mesh,
        in_specs=(P("dp", "ctx"), P(), P(), P(), P(), P(), P("dp", None, "ctx")),
        out_specs=(P("dp", None, "ctx"), P(), P()),
        check_vma=False,
    )
```

```python
import functools
import math

import jax
import jax.numpy as jnp
import numpy as np
from jax import lax
from jax.experimental import pallas as pl
from jax.experimental.pallas import tpu as pltpu
from jax.sharding import PartitionSpec as P

F32 = jnp.float32
BF16 = jnp.bfloat16
GROUP = 256
SUBLANES = 8
LANES = 128
BESIDE = 4


def xor_permute(block, axis, mask):
    size = math.prod(lax.axis_size(name) for name in axis)
    return lax.ppermute(block, axis, [(i, i ^ mask) for i in range(size)])


def masks_of(size):
    return [1 << bit for bit in range(size.bit_length() - 1)]


def halves(table):
    upper = table.astype(BF16)
    return upper, (table - upper.astype(F32)).astype(BF16)


def dot(left, right):
    return jnp.dot(left, right, preferred_element_type=F32)


def row_token(row, block_len):
    return row % SUBLANES * (block_len // SUBLANES) + row // SUBLANES


def order_matrix(block_len, transposed=False):
    row = lax.broadcasted_iota(jnp.int32, (block_len, block_len), 1 if transposed else 0)
    token = lax.broadcasted_iota(jnp.int32, (block_len, block_len), 0 if transposed else 1)
    return jnp.where(row_token(row, block_len) == token, 1.0, 0.0).astype(BF16)


def dft_tables(block_len):
    period = 2 * block_len
    column = np.arange(block_len)[:, None]
    row = np.arange(block_len)
    sample = np.concatenate([row_token(row, block_len), block_len + row_token(row, block_len)])[None, :]
    angle = (column * sample % period) * (2.0 * math.pi / period)
    parity = 1.0 - 2.0 * (sample % 2)
    imag = np.where(column == 0, parity, -np.sin(angle))
    forward = np.concatenate([np.cos(angle), imag], axis=0)
    weight = np.where(np.arange(period) % block_len == 0, 1.0, 2.0) / period
    inverse = (forward[:, :block_len] * weight[:, None]).T
    return forward, inverse


def row_delays(block_len, seq_len, row):
    token = row_token(row % block_len, block_len) + row // block_len * block_len
    period = 2 * block_len
    body = seq_len - block_len

    def near(n):
        return n + (n >= block_len) * (seq_len - period)

    return near, lambda n: body - n, lambda n: n, token


def mode_constants(block_len, seq_len, modes):
    parts = []
    for at, length in enumerate((2 * block_len, seq_len - block_len, block_len)):
        delays = row_delays(block_len, seq_len, np.arange(length))
        parts.append(delays[at](delays[3]))
    delay = np.concatenate(parts)[:, None]
    period = 2 * modes + 2
    angle = (delay * (np.arange(modes)[None, :] + 1) % period) * (2.0 * math.pi / period)
    ratio = delay / seq_len
    parts = [np.cos(angle), np.sin(angle), -ratio * np.cos(angle), -ratio * np.sin(angle)]
    wave = np.concatenate(parts, axis=1)
    return np.pad(wave, ((0, 0), (0, LANES - wave.shape[1]))).astype(np.float32)


def tables_kernel(modes, block_len, seq_len, *refs):
    sources, outs, scratch = refs[:7], refs[7:16], refs[16:]
    ids_out, grad_t_ref, short_out, res_out, fwd_out, far_ref, here_ref, near_ref, spec_ref = outs
    few, rate_row, wave, fwd, grad, copied = scratch
    targets = [few, wave, fwd, grad, ids_out, res_out, short_out]
    pairs = list(zip(sources, targets, strict=True))
    copies = [pltpu.make_async_copy(*pair, copied.at[i]) for i, pair in enumerate(pairs)]
    for copy in copies:
        copy.start()
    rate_row[...] = jnp.zeros_like(rate_row)
    period = 2 * block_len
    body = seq_len - block_len
    copies[0].wait()
    rate_row[:, :modes] = few[...]
    rates = rate_row[...]
    for shift in (modes, 2 * modes):
        rates = rates + pltpu.roll(rates, shift, 1)

    def decay_of(at, length):
        delays = row_delays(block_len, seq_len, lax.broadcasted_iota(jnp.int32, (length, LANES), 0))
        delay = delays[at](delays[3]).astype(F32)
        return jnp.exp(delay * (-1.0 / seq_len) * rates)

    near = decay_of(0, period)
    far = decay_of(1, body)
    here = decay_of(2, block_len)
    copies[1].wait()
    near = near * wave[:period]
    far = far * wave[period : period + body]
    here = here * wave[period + body :]
    used = 4 * modes
    near_hi, near_lo = halves(near)
    copies[2].wait()
    fwd_hi, fwd_lo = halves(fwd[...])
    spec = dot(fwd_hi, near_hi) + dot(fwd_hi, near_lo) + dot(fwd_lo, near_hi)
    fwd_out[:period, :] = fwd_hi[:, :block_len]
    fwd_out[period:, :] = fwd_lo[:, :block_len]
    spec_ref[:period, :] = spec
    spec_ref[period:, :] = here
    far_ref[...] = jnp.concatenate(halves(far.T[:used]), axis=0)
    here_ref[...] = jnp.concatenate(halves(here.T[:used]), axis=0)
    place = lax.broadcasted_iota(jnp.int32, (period, LANES), 0)
    weight = jnp.where(lax.rem(place, block_len) == 0, 1.0 / period, 2.0 / period)
    spec_t = (spec * weight).T
    grad_rows = jnp.concatenate([spec_t[:modes], spec_t[2 * modes : 3 * modes]], axis=0)
    near_ref[...] = jnp.concatenate(halves(grad_rows), axis=0)
    copies[3].wait()
    grad_t_ref[...] = lax.dot_general(
        order_matrix(block_len), grad[...], (((1,), (1,)), ((), ())), preferred_element_type=F32
    )
    for copy in copies[4:]:
        copy.wait()


def main_kernel(modes, blocks, block_len, taps, channels, table_ref, short_ref, res_ref, fwd_ref, far_ref, here_ref,
                near_ref, grad_t_ref, *refs):
    bits = blocks.bit_length() - 1
    ids_refs, refs = refs[: bits + 1], refs[bits + 1 :]
    part_ref, rate_ref, query_ref, gated_ref, spec_ref, state_ref, onehot, ids = refs
    groups = channels // GROUP
    filled = 0
    for ref in ids_refs:
        ids[filled : filled + ref.shape[0], :] = ref[...]
        filled += ref.shape[0]
    seq_len = blocks * block_len
    vocab = table_ref.shape[1]
    own = lax.axis_index("ctx")
    order = order_matrix(block_len)
    order = jnp.concatenate([order * 16, order], axis=1)
    lane = lax.broadcasted_iota(jnp.int32, (block_len, LANES), 1).astype(F32)
    for place in range(blocks):
        source = lax.rem(own + 1 + place, blocks)
        flags = [((source ^ own) >> bit) & 1 for bit in range(bits)]
        slot = sum(flag << (bits - 1 - bit) for bit, flag in enumerate(flags) if bit > 0)
        slot = slot | (functools.reduce(lambda a, b: a ^ b, flags) << (bits - 1))
        row = ids[pl.ds(slot, 1), :]
        digits = jnp.concatenate([row >> 4, row & 15], axis=1).astype(F32)
        digits = jnp.broadcast_to(digits, (LANES, 2 * block_len)).astype(BF16)
        column = lax.dot_general(order, digits, (((1,), (1,)), ((), ())), preferred_element_type=F32)
        for piece in range(vocab // LANES):
            onehot[pl.ds(place * block_len, block_len), pl.ds(piece * LANES, LANES)] = jnp.where(
                column == lane + float(piece * LANES), 1.0, 0.0
            ).astype(BF16)
    body = seq_len - block_len
    period = 2 * block_len
    halo = SUBLANES * (taps - 1)
    rate = jnp.zeros((modes, 1), F32)
    last = lax.broadcasted_iota(jnp.int32, (halo, GROUP), 0) % SUBLANES == SUBLANES - 1

    def gather(group, part, rows):
        block = table_ref[pl.ds(part * channels + group * GROUP, GROUP), :]
        return lax.dot_general(onehot[rows:, :], block, (((1,), (1,)), ((), ())), preferred_element_type=F32)

    def features(group):
        return gather(group, 0, body - halo), gather(group, 1, 0), gather(group, 2, 0)

    def short_conv(tail, block, rows):
        own_tail = block[block_len - halo :]
        ahead = jnp.where(last, tail, own_tail).reshape(taps - 1, SUBLANES, GROUP)
        ahead = pltpu.roll(ahead, 1, 1).reshape(halo, GROUP)
        padded = jnp.concatenate([ahead, block], axis=0)
        total = None
        for tap in range(taps):
            weight = short_ref[tap : tap + 1, pl.ds(rows, GROUP)]
            term = weight * padded[tap * SUBLANES : tap * SUBLANES + block_len]
            total = term if total is None else total + term
        return total

    def one_group(group, own_query, rate):
        base = group * GROUP
        own_query, keys, vals = own_query
        query = short_conv(own_query[:halo], own_query[halo:], base)
        gated = []
        for place in range(blocks):
            at = place * block_len
            before = (at - halo) % seq_len
            mixes = [
                short_conv(feat[before : before + halo], feat[at : at + block_len], rows)
                for feat, rows in ((keys, channels + base), (vals, 2 * channels + base))
            ]
            gated.append((mixes[0] * mixes[1]).astype(BF16))
        gated = jnp.concatenate(gated, axis=0)
        span = pl.ds(base, GROUP)
        query_ref[:, span] = query
        gated_own = gated[body:]
        gated_ref[:, span] = gated_own
        dconv = query * grad_t_ref[:, span]
        dconv_both = jnp.concatenate(halves(dconv), axis=0)
        spec = dot(fwd_ref[...], gated_own)
        spec = spec[:period] + spec[period:]
        spec_ref[:, span] = spec
        left = jnp.concatenate([fwd_ref[...], here_ref[...]], axis=0)
        dspec = dot(jnp.concatenate([left, left], axis=1), dconv_both)
        dstate = dspec[2 * period :]
        dspec = dspec[:period] + dspec[period : 2 * period]
        dstate = dstate[: 4 * modes] + dstate[4 * modes :]
        state = dot(far_ref[...], gated[:body])
        state = state[: 4 * modes] + state[4 * modes :]
        left_re, left_im = spec[:block_len], spec[block_len:]
        right_re, right_im = dspec[:block_len], dspec[block_len:]
        leading = lax.broadcasted_iota(jnp.int32, (block_len, GROUP), 0) == 0
        rere, imim = left_re * right_re, left_im * right_im
        cross_re = jnp.where(leading, rere, rere + imim)
        cross_im = jnp.where(leading, imim, left_re * right_im - left_im * right_re)
        cross = jnp.concatenate([cross_re, cross_im], axis=0)
        cross_hi, cross_lo = halves(cross)
        near = near_ref[...]
        terms = dot(near, cross_hi) + dot(near, cross_lo)
        terms = terms[: 2 * modes] + terms[2 * modes :]
        sc, ss, sc1, ss1 = (state[i * modes : (i + 1) * modes] for i in range(4))
        dc, ds, dc1, ds1 = (dstate[i * modes : (i + 1) * modes] for i in range(4))
        grad = terms[:modes] + dc * sc - ds * ss
        slope = terms[modes:] + dc1 * sc + dc * sc1 - ds1 * ss - ds * ss1
        res = res_ref[:, span]
        state_ref[:modes, span] = res * sc
        state_ref[modes:, span] = -(res * ss)
        for side in range(GROUP // LANES):
            at = (base + side * LANES) // LANES * modes
            part_ref[pl.ds(at, modes), :] = grad[:, side * LANES : (side + 1) * LANES]
        return rate + jnp.sum(res * slope, axis=1, keepdims=True)

    own_query = features(0)
    for group in range(groups):
        ahead = features(group + 1) if group + 1 < groups else None
        rate = one_group(group, own_query, rate)
        own_query = ahead
    wide = jnp.broadcast_to(rate, (modes, LANES))
    square = jnp.concatenate([wide, jnp.zeros((LANES - modes, LANES), F32)], axis=0).T
    rate_ref[...] = square[:8]


def filter_kernel(modes, block_len, spec_ref, res_ref, inv_ref, skip_ref, filt_ref, inv_out, skip_out, inv, copied):
    copies = [
        pltpu.make_async_copy(inv_ref, inv, copied.at[0]),
        pltpu.make_async_copy(skip_ref, skip_out, copied.at[1]),
    ]
    for copy in copies:
        copy.start()
    period = 2 * block_len
    spec_hi, spec_lo = halves(spec_ref[:period, :modes])
    res_hi, res_lo = halves(res_ref[...])
    left = jnp.concatenate([spec_hi, spec_hi, spec_lo], axis=1)
    filt_ref[...] = dot(left, jnp.concatenate([res_hi, res_lo, res_hi], axis=0))
    for copy in copies:
        copy.wait()
    inv_out[:, :period] = inv[...].astype(BF16)
    inv_out[:, period:] = spec_ref[period:, : 2 * modes].astype(BF16)


def mixed_kernel(block_len, query_ref, gated_ref, spec_ref, filt_ref, state_ref, inv_ref, skip_ref, out_ref):
    channels = query_ref.shape[1]
    leading = lax.broadcasted_iota(jnp.int32, (block_len, GROUP), 0) == 0
    order = order_matrix(block_len, True)
    inv = inv_ref[...]
    for base in range(0, channels, GROUP):
        span = pl.ds(base, GROUP)
        left_re, left_im = filt_ref[:block_len, span], filt_ref[block_len:, span]
        right_re, right_im = spec_ref[:block_len, span], spec_ref[block_len:, span]
        rere, imim = left_re * right_re, left_im * right_im
        out_re = jnp.where(leading, rere, rere - imim)
        out_im = jnp.where(leading, imim, left_re * right_im + left_im * right_re)
        conv = dot(inv, jnp.concatenate([out_re, out_im, state_ref[:, span]], axis=0).astype(BF16))
        mixed = query_ref[:, span] * (conv + skip_ref[:, span] * gated_ref[:, span].astype(F32))
        mixed = dot(order, mixed.astype(BF16))
        out_ref[pl.ds(base, GROUP), :] = mixed.T.astype(BF16)


def call(kernel, outs, scratch, args, cost, spaces=None):
    return pl.pallas_call(
        kernel,
        out_shape=[jax.ShapeDtypeStruct(shape, dtype) for shape, dtype in outs],
        in_specs=[pl.BlockSpec(memory_space=space) for space in spaces or [pltpu.VMEM] * len(args)],
        out_specs=[pl.BlockSpec(memory_space=pltpu.VMEM)] * len(outs),
        scratch_shapes=scratch,
        compiler_params=pltpu.CompilerParams(vmem_limit_bytes=40 * 1024 * 1024),
        cost_estimate=pl.CostEstimate(flops=cost[0], bytes_accessed=cost[1], transcendentals=0),
    )(*args)


def sum_kernel(modes, part_ref, moved_ref, grad_ref, rate_ref):
    tiles = grad_ref.shape[1] // LANES
    for tile in range(tiles):
        rows = pl.ds(tile * modes, modes)
        grad_ref[:, tile * LANES : (tile + 1) * LANES] = part_ref[rows, :] + moved_ref[rows, :].astype(F32)
    rest = moved_ref[tiles * modes : tiles * modes + 16, :].astype(F32)
    rate = part_ref[tiles * modes : tiles * modes + 1, :] + (rest[:1] + rest[1:2])
    rate_ref[...] = rate[:, :modes]


def rounded(value):
    return lax.reduce_precision(value, 8, 7)


def per_device(token_ids, feature_table, short_weight, residue, rates, skip_gain, grad_out):
    block_len = token_ids.shape[1]
    blocks = lax.axis_size("ctx")
    seq_len = block_len * blocks
    channels, modes = residue.shape
    taps = short_weight.shape[1]
    vocab = feature_table.shape[1]
    period = 2 * block_len
    forward, inverse = dft_tables(block_len)
    wave = mode_constants(block_len, seq_len, modes)
    rows = channels // LANES * modes

    masks = [mask | 1 for mask in masks_of(blocks)[:0:-1]] + [1]
    moved_ids = [xor_permute(token_ids, ("ctx",), masks[0])]
    def in_hbm(*arrays):
        return [pltpu.with_memory_space_constraint(array, pltpu.HBM) for array in arrays]

    vmem, hbm = pltpu.VMEM, pltpu.HBM
    ids, grad_t, short, res, fwd, far, here, near, table_spec = call(
        functools.partial(tables_kernel, modes, block_len, seq_len),
        [
            ((1, block_len), jnp.int32),
            ((block_len, channels), F32),
            (short_weight.shape[::-1], F32),
            ((modes, channels), F32),
            ((2 * period, block_len), BF16),
            ((8 * modes, seq_len - block_len), BF16),
            ((8 * modes, block_len), BF16),
            ((4 * modes, period), BF16),
            ((period + block_len, LANES), F32),
        ],
        [
            vmem((1, modes), F32),
            vmem((1, LANES), F32),
            vmem(wave.shape, F32),
            vmem(forward.shape, F32),
            vmem(grad_out.shape[1:], BF16),
            pltpu.SemaphoreType.DMA((7,)),
        ],
        in_hbm(
            rates[None],
            jnp.asarray(wave),
            jnp.asarray(forward.astype(np.float32)),
            grad_out[0],
            token_ids,
            residue.T,
            short_weight.T,
        ),
        (10_000_000_000, 40_000_000),
        [hbm] * 7,
    )
    for mask in masks[1:]:
        moved_ids.append(xor_permute(jnp.concatenate([ids, *moved_ids], axis=0), ("ctx",), mask))
    part, rate, query, gated, spec, state = call(
        functools.partial(main_kernel, modes, blocks, block_len, taps, channels),
        [
            ((rows, LANES), F32),
            ((8, LANES), F32),
            ((block_len, channels), F32),
            ((block_len, channels), BF16),
            ((period, channels), F32),
            ((2 * modes, channels), F32),
        ],
        [
            vmem((seq_len, vocab), BF16),
            vmem((blocks, block_len), jnp.int32),
        ],
        [feature_table, short, res, fwd, far, here, near, grad_t, ids, *moved_ids],
        (2 * seq_len * vocab * 3 * channels, 6_000_000),
    )
    core = lax.axis_size("dp")
    stages = [core] + [mask | core for mask in masks_of(blocks * core) if mask != core]
    filler = jnp.zeros((14, LANES), BF16)
    for stage in stages:
        part = rounded(part)
        upper = rounded(rate[:1])
        lower = rounded(rate[:1] - upper)
        sent = jnp.concatenate([part.astype(BF16), upper.astype(BF16), lower.astype(BF16), filler], axis=0)
        if stage == stages[1]:
            sent, res = lax.optimization_barrier((sent, res))
            filt, inv, skip = call(
                functools.partial(filter_kernel, modes, block_len),
                [((period, channels), F32), ((block_len, period + 2 * modes), BF16), ((1, channels), F32)],
                [vmem(inverse.shape, F32), pltpu.SemaphoreType.DMA((2,))],
                [table_spec, res, *in_hbm(jnp.asarray(inverse.astype(np.float32)), skip_gain[None])],
                (50_000_000, 1_500_000),
                [vmem, vmem, hbm, hbm],
            )
        if stage == stages[BESIDE]:
            sent, query = lax.optimization_barrier((sent, query))
            (mixed,) = call(
                functools.partial(mixed_kernel, block_len),
                [((channels, block_len), BF16)],
                [],
                [query, gated, spec, filt, state, inv, skip],
                (300_000_000, 3_000_000),
            )
        moved = xor_permute(sent, ("ctx", "dp"), stage)
        if stage != stages[-1]:
            part = part + moved[:rows].astype(F32)
            rate = upper + lower + (moved[rows : rows + 1].astype(F32) + moved[rows + 1 : rows + 2].astype(F32))
    kept = jnp.concatenate([part, upper + lower], axis=0)
    grad, rate = call(
        functools.partial(sum_kernel, modes),
        [((modes, channels), F32), ((1, modes), F32)],
        [],
        [kept, moved],
        (0, 200_000),
    )
    return (mixed[None], grad.T, rate[0])


def solution(mesh):
    return jax.shard_map(
        per_device,
        mesh=mesh,
        in_specs=(P("dp", "ctx"), P(), P(), P(), P(), P(), P("dp", None, "ctx")),
        out_specs=(P("dp", None, "ctx"), P(), P()),
        check_vma=False,
    )
```

```python
import functools
import math

import jax
import jax.numpy as jnp
import numpy as np
from jax import lax
from jax.experimental import pallas as pl
from jax.experimental.pallas import tpu as pltpu
from jax.sharding import PartitionSpec as P

F32 = jnp.float32
BF16 = jnp.bfloat16
GROUP = 256
WIDE = 2 * GROUP
SUBLANES = 8
LANES = 128


def xor_permute(block, axis, mask):
    size = math.prod(lax.axis_size(name) for name in axis)
    return lax.ppermute(block, axis, [(i, i ^ mask) for i in range(size)])


def masks_of(size):
    return [1 << bit for bit in range(size.bit_length() - 1)]


def half_index():
    bits = lax.axis_index("ctx") ^ lax.axis_index("dp")
    for shift in (4, 2, 1):
        bits = bits ^ (bits >> shift)
    return bits & 1


def halves(table):
    upper = table.astype(BF16)
    return upper, (table - upper.astype(F32)).astype(BF16)


def dot(left, right):
    return jnp.dot(left, right, preferred_element_type=F32)


def row_token(row, block_len):
    return row % SUBLANES * (block_len // SUBLANES) + row // SUBLANES


def order_matrix(block_len, transposed=False):
    row = lax.broadcasted_iota(jnp.int32, (block_len, block_len), 1 if transposed else 0)
    token = lax.broadcasted_iota(jnp.int32, (block_len, block_len), 0 if transposed else 1)
    return jnp.where(row_token(row, block_len) == token, 1.0, 0.0).astype(BF16)


def dft_tables(block_len):
    period = 2 * block_len
    column = np.arange(block_len)[:, None]
    row = np.arange(block_len)
    sample = np.concatenate([row_token(row, block_len), block_len + row_token(row, block_len)])[None, :]
    angle = (column * sample % period) * (2.0 * math.pi / period)
    parity = 1.0 - 2.0 * (sample % 2)
    imag = np.where(column == 0, parity, -np.sin(angle))
    forward = np.concatenate([np.cos(angle), imag], axis=0)
    weight = np.where(np.arange(period) % block_len == 0, 1.0, 2.0) / period
    inverse = (forward[:, :block_len] * weight[:, None]).T
    return forward, inverse


def row_delays(block_len, seq_len, row):
    token = row_token(row % block_len, block_len) + row // block_len * block_len
    period = 2 * block_len
    body = seq_len - block_len

    def near(n):
        return n + (n >= block_len) * (seq_len - period)

    return near, lambda n: body - n, lambda n: n, token


def mode_constants(block_len, seq_len, modes):
    parts = []
    for at, length in enumerate((2 * block_len, seq_len - block_len, block_len)):
        delays = row_delays(block_len, seq_len, np.arange(length))
        parts.append(delays[at](delays[3]))
    delay = np.concatenate(parts)[:, None]
    period = 2 * modes + 2
    angle = (delay * (np.arange(modes)[None, :] + 1) % period) * (2.0 * math.pi / period)
    ratio = delay / seq_len
    parts = [np.cos(angle), np.sin(angle), -ratio * np.cos(angle), -ratio * np.sin(angle)]
    wave = np.concatenate(parts, axis=1)
    return np.pad(wave, ((0, 0), (0, LANES - wave.shape[1]))).astype(np.float32)


def tables_kernel(modes, block_len, seq_len, *refs):
    sources, outs, scratch = refs[:6], refs[6:14], refs[14:]
    ids_out, short_out, res_out, fwd_out, far_ref, here_ref, near_ref, spec_ref = outs
    few, rate_row, wave, fwd, copied = scratch
    targets = [few, wave, fwd, ids_out, res_out, short_out]
    pairs = list(zip(sources, targets, strict=True))
    copies = [pltpu.make_async_copy(*pair, copied.at[i]) for i, pair in enumerate(pairs)]
    for copy in copies:
        copy.start()
    rate_row[...] = jnp.zeros_like(rate_row)
    period = 2 * block_len
    body = seq_len - block_len
    copies[0].wait()
    rate_row[:, :modes] = few[...]
    rates = rate_row[...]
    for shift in (modes, 2 * modes):
        rates = rates + pltpu.roll(rates, shift, 1)

    def decay_of(at, length):
        delays = row_delays(block_len, seq_len, lax.broadcasted_iota(jnp.int32, (length, LANES), 0))
        delay = delays[at](delays[3]).astype(F32)
        return jnp.exp(delay * (-1.0 / seq_len) * rates)

    near = decay_of(0, period)
    far = decay_of(1, body)
    here = decay_of(2, block_len)
    copies[1].wait()
    near = near * wave[:period]
    far = far * wave[period : period + body]
    here = here * wave[period + body :]
    used = 4 * modes
    near_hi, near_lo = halves(near)
    copies[2].wait()
    fwd_hi, fwd_lo = halves(fwd[...])
    spec = dot(fwd_hi, near_hi) + dot(fwd_hi, near_lo) + dot(fwd_lo, near_hi)
    fwd_out[:period, :] = fwd_hi[:, :block_len]
    fwd_out[period:, :] = fwd_lo[:, :block_len]
    spec_ref[:period, :] = spec
    spec_ref[period:, :] = here
    far_ref[...] = jnp.concatenate(halves(far.T[:used]), axis=0)
    here_ref[...] = jnp.concatenate(halves(here.T[:used]), axis=0)
    place = lax.broadcasted_iota(jnp.int32, (period, LANES), 0)
    weight = jnp.where(lax.rem(place, block_len) == 0, 1.0 / period, 2.0 / period)
    spec_t = (spec * weight).T
    grad_rows = jnp.concatenate([spec_t[:modes], spec_t[2 * modes : 3 * modes]], axis=0)
    near_ref[...] = jnp.concatenate(halves(grad_rows), axis=0)
    for copy in copies[3:]:
        copy.wait()


def main_kernel(modes, blocks, block_len, taps, channels, table_ref, short_ref, res_ref, fwd_ref, far_ref, here_ref,
                near_ref, grad_ref, mate_ref, *refs):
    bits = blocks.bit_length() - 1
    ids_refs, refs = refs[: bits + 1], refs[bits + 1 :]
    part_ref, query_ref, gated_ref, spec_ref, state_ref, onehot, ids = refs
    half = channels // 2
    groups = half // GROUP
    first = half_index() * half
    filled = 0
    for ref in ids_refs:
        ids[filled : filled + ref.shape[0], :] = ref[...]
        filled += ref.shape[0]
    seq_len = blocks * block_len
    vocab = table_ref.shape[1]
    own = lax.axis_index("ctx")
    order_one = order_matrix(block_len)
    order = jnp.concatenate([order_one * 16, order_one], axis=1)
    on_hi = (own & 1) == 1
    lane = lax.broadcasted_iota(jnp.int32, (block_len, LANES), 1).astype(F32)
    for place in range(blocks):
        source = lax.rem((own & -2) + 2 + place, blocks)
        flags = [((source ^ own) >> bit) & 1 for bit in range(bits)]
        slot = sum(flag << (bits - 1 - bit) for bit, flag in enumerate(flags) if bit > 0)
        slot = slot | (functools.reduce(lambda a, b: a ^ b, flags) << (bits - 1))
        row = ids[pl.ds(slot, 1), :]
        digits = jnp.concatenate([row >> 4, row & 15], axis=1).astype(F32)
        digits = jnp.broadcast_to(digits, (LANES, 2 * block_len)).astype(BF16)
        column = lax.dot_general(order, digits, (((1,), (1,)), ((), ())), preferred_element_type=F32)
        for piece in range(vocab // LANES):
            onehot[pl.ds(place * block_len, block_len), pl.ds(piece * LANES, LANES)] = jnp.where(
                column == lane + float(piece * LANES), 1.0, 0.0
            ).astype(BF16)
    body = seq_len - block_len
    period = 2 * block_len
    halo = SUBLANES * (taps - 1)
    rate = jnp.zeros((modes, 1), F32)
    last = lax.broadcasted_iota(jnp.int32, (halo, GROUP), 0) % SUBLANES == SUBLANES - 1

    def gather(group, part, rows):
        block = table_ref[pl.ds(pl.multiple_of(first + part * channels + group * GROUP, GROUP), GROUP), :]
        return lax.dot_general(onehot[rows:, :], block, (((1,), (1,)), ((), ())), preferred_element_type=F32)

    def features(group):
        return gather(group, 0, body - block_len - halo), gather(group, 1, 0), gather(group, 2, 0)

    def short_conv(feat, at, weights):
        tail = feat[(at - halo) % feat.shape[0] :][:halo]
        block = feat[at : at + block_len]
        ahead = jnp.where(last, tail, block[block_len - halo :]).reshape(taps - 1, SUBLANES, GROUP)
        ahead = pltpu.roll(ahead, 1, 1).reshape(halo, GROUP)
        padded = jnp.concatenate([ahead, block], axis=0)
        total = None
        for tap in range(taps):
            term = weights[tap : tap + 1] * padded[tap * SUBLANES : tap * SUBLANES + block_len]
            total = term if total is None else total + term
        return total

    def one_group(group, feats, rate):
        weights = [
            short_ref[:, pl.ds(pl.multiple_of(first + part * channels + group * GROUP, GROUP), GROUP)]
            for part in range(3)
        ]
        query = [short_conv(feats[0], halo + at, weights[0]) for at in (0, block_len)]
        query = jnp.concatenate(query, axis=1)
        gated = []
        for place in range(blocks):
            keys, vals = (short_conv(feats[part], place * block_len, weights[part]) for part in (1, 2))
            gated.append((keys * vals).astype(BF16))
        ahead_lo = jnp.concatenate([gated[-1], *gated[:-2]], axis=0)
        gated_far = jnp.concatenate([ahead_lo, jnp.concatenate(gated[:-1], axis=0)], axis=1)
        gated_own = jnp.concatenate(gated[-2:], axis=1)
        span = pl.ds(group * WIDE, WIDE)
        query_ref[:, span] = query
        gated_ref[:, span] = gated_own
        rows = pl.ds(pl.multiple_of(first + group * GROUP, GROUP), GROUP)
        own_grad, mate_grad = grad_ref[rows, :], mate_ref[rows, :]
        grads = jnp.concatenate(
            [jnp.where(on_hi, mate_grad, own_grad), jnp.where(on_hi, own_grad, mate_grad)], axis=0
        )
        grads = lax.dot_general(order_one, grads, (((1,), (1,)), ((), ())), preferred_element_type=F32)
        dconv = query * grads
        dconv_both = jnp.concatenate(halves(dconv), axis=0)
        spec = dot(fwd_ref[...], gated_own)
        spec = spec[:period] + spec[period:]
        spec_ref[:, span] = spec
        left = jnp.concatenate([fwd_ref[...], here_ref[...]], axis=0)
        dspec = dot(jnp.concatenate([left, left], axis=1), dconv_both)
        dstate = dspec[2 * period :]
        dspec = dspec[:period] + dspec[period : 2 * period]
        dstate = dstate[: 4 * modes] + dstate[4 * modes :]
        state = dot(far_ref[...], gated_far)
        state = state[: 4 * modes] + state[4 * modes :]
        left_re, left_im = spec[:block_len], spec[block_len:]
        right_re, right_im = dspec[:block_len], dspec[block_len:]
        leading = lax.broadcasted_iota(jnp.int32, (block_len, WIDE), 0) == 0
        rere, imim = left_re * right_re, left_im * right_im
        cross_re = jnp.where(leading, rere, rere + imim)
        cross_im = jnp.where(leading, imim, left_re * right_im - left_im * right_re)
        cross = jnp.concatenate([cross_re, cross_im], axis=0)
        cross_hi, cross_lo = halves(cross)
        near = near_ref[...]
        terms = dot(near, cross_hi) + dot(near, cross_lo)
        terms = terms[: 2 * modes] + terms[2 * modes :]
        sc, ss, sc1, ss1 = (state[i * modes : (i + 1) * modes] for i in range(4))
        dc, ds, dc1, ds1 = (dstate[i * modes : (i + 1) * modes] for i in range(4))
        grad = terms[:modes] + dc * sc - ds * ss
        slope = terms[modes:] + dc1 * sc + dc * sc1 - ds1 * ss - ds * ss1
        res = res_ref[:, pl.ds(pl.multiple_of(first + group * GROUP, GROUP), GROUP)]
        both = jnp.concatenate([res, res], axis=1)
        state_ref[:modes, span] = both * sc
        state_ref[modes:, span] = -(both * ss)
        grad = grad[:, :GROUP] + grad[:, GROUP:]
        slope = slope[:, :GROUP] + slope[:, GROUP:]
        for side in range(GROUP // LANES):
            at = (group * GROUP + side * LANES) // LANES * modes
            part_ref[pl.ds(at, modes), :] = grad[:, side * LANES : (side + 1) * LANES]
        return rate + jnp.sum(res * slope, axis=1, keepdims=True)

    feats = features(0)
    for group in range(groups):
        ahead = features(group + 1) if group + 1 < groups else None
        rate = one_group(group, feats, rate)
        feats = ahead
    wide = jnp.broadcast_to(rate, (modes, LANES))
    square = jnp.concatenate([wide, jnp.zeros((LANES - modes, LANES), F32)], axis=0).T
    part_ref[pl.ds(half // LANES * modes, SUBLANES), :] = square[:SUBLANES]


def filter_kernel(modes, block_len, spec_ref, res_ref, inv_ref, skip_ref, filt_ref, inv_out, skip_out, inv, copied):
    copies = [
        pltpu.make_async_copy(inv_ref, inv, copied.at[0]),
        pltpu.make_async_copy(skip_ref, skip_out, copied.at[1]),
    ]
    for copy in copies:
        copy.start()
    period = 2 * block_len
    spec_hi, spec_lo = halves(spec_ref[:period, :modes])
    half = res_ref.shape[1] // 2
    res_hi, res_lo = halves(res_ref[:, pl.ds(pl.multiple_of(half_index() * half, half), half)])
    left = jnp.concatenate([spec_hi, spec_hi, spec_lo], axis=1)
    filt_ref[...] = dot(left, jnp.concatenate([res_hi, res_lo, res_hi], axis=0))
    for copy in copies:
        copy.wait()
    inv_out[:, :period] = inv[...].astype(BF16)
    inv_out[:, period:] = spec_ref[period:, : 2 * modes].astype(BF16)


def mixed_kernel(block_len, query_ref, gated_ref, spec_ref, filt_ref, state_ref, inv_ref, skip_ref, own_ref, mate_ref):
    half = filt_ref.shape[1]
    first = half_index() * half
    on_hi = (lax.axis_index("ctx") & 1) == 1
    leading = lax.broadcasted_iota(jnp.int32, (block_len, WIDE), 0) == 0
    order = order_matrix(block_len, True)
    inv = inv_ref[...]
    for group in range(half // GROUP):
        span = pl.ds(group * WIDE, WIDE)
        rows = pl.ds(group * GROUP, GROUP)
        filt = filt_ref[:, rows]
        filt = jnp.concatenate([filt, filt], axis=1)
        skip = skip_ref[:, pl.ds(pl.multiple_of(first + group * GROUP, GROUP), GROUP)]
        left_re, left_im = filt[:block_len], filt[block_len:]
        right_re, right_im = spec_ref[:block_len, span], spec_ref[block_len:, span]
        rere, imim = left_re * right_re, left_im * right_im
        out_re = jnp.where(leading, rere, rere - imim)
        out_im = jnp.where(leading, imim, left_re * right_im + left_im * right_re)
        conv = dot(inv, jnp.concatenate([out_re, out_im, state_ref[:, span]], axis=0).astype(BF16))
        through = jnp.concatenate([skip, skip], axis=1) * gated_ref[:, span].astype(F32)
        mixed = dot(order, (query_ref[:, span] * (conv + through)).astype(BF16))
        low, high = mixed[:, :GROUP], mixed[:, GROUP:]
        own_ref[rows, :] = jnp.where(on_hi, high, low).T.astype(BF16)
        mate_ref[rows, :] = jnp.where(on_hi, low, high).T.astype(BF16)


def call(kernel, outs, scratch, args, cost, spaces=None, out_spaces=None):
    return pl.pallas_call(
        kernel,
        out_shape=[jax.ShapeDtypeStruct(shape, dtype) for shape, dtype in outs],
        in_specs=[pl.BlockSpec(memory_space=space) for space in spaces or [pltpu.VMEM] * len(args)],
        out_specs=[pl.BlockSpec(memory_space=space) for space in out_spaces or [pltpu.VMEM] * len(outs)],
        scratch_shapes=scratch,
        compiler_params=pltpu.CompilerParams(vmem_limit_bytes=40 * 1024 * 1024),
        cost_estimate=pl.CostEstimate(flops=cost[0], bytes_accessed=cost[1], transcendentals=0),
    )(*args)


def result_kernel(modes, part_ref, moved_ref, own_ref, mate_ref, grad_ref, rate_ref, mixed_ref, copied):
    half = own_ref.shape[0]
    second = half_index()
    copies = []
    for at, (source, place) in enumerate(((own_ref, second), (mate_ref, 1 - second))):
        target = mixed_ref.at[pl.ds(pl.multiple_of(place * half, half), half)]
        copies.append(pltpu.make_async_copy(source, target, copied.at[at]))
    for copy in copies:
        copy.start()
    for tile in range(half // LANES):
        rows = pl.ds(tile * modes, modes)
        part, moved = part_ref[rows, :], moved_ref[rows, :]
        grad_ref[:, pl.ds(tile * LANES, LANES)] = jnp.where(second == 1, moved, part)
        grad_ref[:, pl.ds(half + tile * LANES, LANES)] = jnp.where(second == 1, part, moved)
    last = half // LANES * modes
    rate_ref[...] = (part_ref[last : last + 1, :] + moved_ref[last : last + 1, :])[:, :modes]
    for copy in copies:
        copy.wait()


def per_device(token_ids, feature_table, short_weight, residue, rates, skip_gain, grad_out):
    block_len = token_ids.shape[1]
    blocks = lax.axis_size("ctx")
    seq_len = block_len * blocks
    channels, modes = residue.shape
    taps = short_weight.shape[1]
    vocab = feature_table.shape[1]
    period = 2 * block_len
    forward, inverse = dft_tables(block_len)
    wave = mode_constants(block_len, seq_len, modes)
    half = channels // 2

    masks = [mask | 1 for mask in masks_of(blocks)[:0:-1]] + [1]
    moved_ids = [xor_permute(token_ids, ("ctx",), masks[0])]
    mate_grad = xor_permute(grad_out[0], ("ctx",), 1)

    def in_hbm(*arrays):
        return [pltpu.with_memory_space_constraint(array, pltpu.HBM) for array in arrays]

    vmem, hbm = pltpu.VMEM, pltpu.HBM
    ids, short, res, fwd, far, here, near, table_spec = call(
        functools.partial(tables_kernel, modes, block_len, seq_len),
        [
            ((1, block_len), jnp.int32),
            (short_weight.shape[::-1], F32),
            ((modes, channels), F32),
            ((2 * period, block_len), BF16),
            ((8 * modes, seq_len - block_len), BF16),
            ((8 * modes, block_len), BF16),
            ((4 * modes, period), BF16),
            ((period + block_len, LANES), F32),
        ],
        [
            vmem((1, modes), F32),
            vmem((1, LANES), F32),
            vmem(wave.shape, F32),
            vmem(forward.shape, F32),
            pltpu.SemaphoreType.DMA((6,)),
        ],
        in_hbm(
            rates[None],
            jnp.asarray(wave),
            jnp.asarray(forward.astype(np.float32)),
            token_ids,
            residue.T,
            short_weight.T,
        ),
        (10_000_000_000, 40_000_000),
        [hbm] * 6,
    )
    for mask in masks[1:]:
        moved_ids.append(xor_permute(jnp.concatenate([ids, *moved_ids], axis=0), ("ctx",), mask))
    part, query, gated, spec, state = call(
        functools.partial(main_kernel, modes, blocks, block_len, taps, channels),
        [
            ((half // LANES * modes + SUBLANES, LANES), F32),
            ((block_len, channels), F32),
            ((block_len, channels), BF16),
            ((period, channels), F32),
            ((2 * modes, channels), F32),
        ],
        [
            vmem((seq_len, vocab), BF16),
            vmem((blocks, block_len), jnp.int32),
        ],
        [feature_table, short, res, fwd, far, here, near, grad_out[0], mate_grad, ids, *moved_ids],
        (4 * seq_len * vocab * channels, 6_000_000),
    )
    core = lax.axis_size("dp")
    hops = [mask | core for mask in masks_of(blocks * core) if mask != core]
    for hop in hops:
        if hop == hops[0]:
            part, res = lax.optimization_barrier((part, res))
            filt, inv, skip = call(
                functools.partial(filter_kernel, modes, block_len),
                [((period, half), F32), ((block_len, period + 2 * modes), BF16), ((1, channels), F32)],
                [vmem(inverse.shape, F32), pltpu.SemaphoreType.DMA((2,))],
                [table_spec, res, *in_hbm(jnp.asarray(inverse.astype(np.float32)), skip_gain[None])],
                (50_000_000, 1_500_000),
                [vmem, vmem, hbm, hbm],
            )
        if hop == hops[1]:
            part, query = lax.optimization_barrier((part, query))
            mixed_own, mixed_mate = call(
                functools.partial(mixed_kernel, block_len),
                [((half, block_len), BF16)] * 2,
                [],
                [query, gated, spec, filt, state, inv, skip],
                (300_000_000, 3_000_000),
            )
        if hop == hops[2]:
            part, mixed_mate = lax.optimization_barrier((part, mixed_mate))
            mixed_moved = xor_permute(mixed_mate, ("ctx", "dp"), core)
        part = part + xor_permute(part, ("ctx", "dp"), hop)
    grad, rate, mixed = call(
        functools.partial(result_kernel, modes),
        [((modes, channels), F32), ((1, modes), F32), ((channels, block_len), BF16)],
        [pltpu.SemaphoreType.DMA((2,))],
        [part, xor_permute(part, ("ctx", "dp"), core), mixed_own, mixed_moved],
        (0, 800_000),
        out_spaces=[vmem, vmem, hbm],
    )
    return (mixed[None], grad.T, rate[0])


def solution(mesh):
    return jax.shard_map(
        per_device,
        mesh=mesh,
        in_specs=(P("dp", "ctx"), P(), P(), P(), P(), P(), P("dp", None, "ctx")),
        out_specs=(P("dp", None, "ctx"), P(), P()),
        check_vma=False,
    )
```

```python
import functools
import math

import jax
import jax.numpy as jnp
import numpy as np
from jax import lax
from jax.experimental import pallas as pl
from jax.experimental.pallas import tpu as pltpu
from jax.sharding import PartitionSpec as P

F32 = jnp.float32
BF16 = jnp.bfloat16
GROUP = 256
WIDE = 2 * GROUP
SUBLANES = 8
LANES = 128


def xor_permute(block, axis, mask):
    size = math.prod(lax.axis_size(name) for name in axis)
    return lax.ppermute(block, axis, [(i, i ^ mask) for i in range(size)])


def masks_of(size):
    return [1 << bit for bit in range(size.bit_length() - 1)]


def half_index():
    bits = lax.axis_index("ctx") ^ lax.axis_index("dp")
    for shift in (4, 2, 1):
        bits = bits ^ (bits >> shift)
    return bits & 1


def halves(table):
    upper = table.astype(BF16)
    return upper, (table - upper.astype(F32)).astype(BF16)


def dot(left, right):
    return jnp.dot(left, right, preferred_element_type=F32)


def row_token(row, block_len):
    return row % SUBLANES * (block_len // SUBLANES) + row // SUBLANES


def order_matrix(block_len, transposed=False):
    row = lax.broadcasted_iota(jnp.int32, (block_len, block_len), 1 if transposed else 0)
    token = lax.broadcasted_iota(jnp.int32, (block_len, block_len), 0 if transposed else 1)
    return jnp.where(row_token(row, block_len) == token, 1.0, 0.0).astype(BF16)


def dft_tables(block_len):
    period = 2 * block_len
    column = np.arange(block_len)[:, None]
    row = np.arange(block_len)
    sample = np.concatenate([row_token(row, block_len), block_len + row_token(row, block_len)])[None, :]
    angle = (column * sample % period) * (2.0 * math.pi / period)
    parity = 1.0 - 2.0 * (sample % 2)
    imag = np.where(column == 0, parity, -np.sin(angle))
    forward = np.concatenate([np.cos(angle), imag], axis=0)
    weight = np.where(np.arange(period) % block_len == 0, 1.0, 2.0) / period
    inverse = (forward[:, :block_len] * weight[:, None]).T
    return forward, inverse


def row_delays(block_len, seq_len, row):
    token = row_token(row % block_len, block_len) + row // block_len * block_len
    period = 2 * block_len
    body = seq_len - block_len

    def near(n):
        return n + (n >= block_len) * (seq_len - period)

    return near, lambda n: body - n, lambda n: n, token


def mode_constants(block_len, seq_len, modes):
    parts = []
    for at, length in enumerate((2 * block_len, seq_len - block_len, block_len)):
        delays = row_delays(block_len, seq_len, np.arange(length))
        parts.append(delays[at](delays[3]))
    delay = np.concatenate(parts)[:, None]
    period = 2 * modes + 2
    angle = (delay * (np.arange(modes)[None, :] + 1) % period) * (2.0 * math.pi / period)
    ratio = delay / seq_len
    parts = [np.cos(angle), np.sin(angle), -ratio * np.cos(angle), -ratio * np.sin(angle)]
    wave = np.concatenate(parts, axis=1)
    return np.pad(wave, ((0, 0), (0, LANES - wave.shape[1]))).astype(np.float32)


def inputs_kernel(modes, block_len, seq_len, *refs):
    sources, outs, scratch = refs[:7], refs[7:14], refs[14:]
    ids_out, short_out, res_out, fwd_out, table_ref, keep_ref, send_ref = outs
    few, rate_row, wave, copied = scratch
    half = keep_ref.shape[0]
    second = half_index()
    grads = [sources[6].at[pl.ds(pl.multiple_of(place * half, half), half)] for place in (1 - second, second)]
    targets = [few, wave, send_ref, fwd_out, ids_out, res_out, short_out, keep_ref]
    pairs = zip([*sources[:2], grads[0], *sources[2:6], grads[1]], targets, strict=True)
    copies = [pltpu.make_async_copy(*pair, copied.at[i]) for i, pair in enumerate(pairs)]
    for copy in copies:
        copy.start()
    rate_row[...] = jnp.zeros_like(rate_row)
    copies[0].wait()
    rate_row[:, :modes] = few[...]
    rates = rate_row[...]
    for shift in (modes, 2 * modes):
        rates = rates + pltpu.roll(rates, shift, 1)
    start = 0
    decays = []
    for at, length in enumerate((2 * block_len, seq_len - block_len, block_len)):
        delays = row_delays(block_len, seq_len, lax.broadcasted_iota(jnp.int32, (length, LANES), 0))
        decays.append(jnp.exp(delays[at](delays[3]).astype(F32) * (-1.0 / seq_len) * rates))
    copies[1].wait()
    for decay in decays:
        rows = pl.ds(start, decay.shape[0])
        table_ref[rows, :] = decay * wave[rows, :]
        start += decay.shape[0]
    for copy in copies[2:]:
        copy.wait()


def tables_kernel(modes, block_len, table_ref, fwd_ref, fwd_out, far_ref, here_ref, near_ref, spec_ref):
    period = 2 * block_len
    used = 4 * modes
    near_hi, near_lo = halves(table_ref[:period, :])
    fwd_hi, fwd_lo = halves(fwd_ref[...])
    spec = dot(fwd_hi, near_hi) + dot(fwd_hi, near_lo) + dot(fwd_lo, near_hi)
    fwd_out[:period, :] = fwd_hi[:, :block_len]
    fwd_out[period:, :] = fwd_lo[:, :block_len]
    spec_ref[...] = spec
    body = table_ref.shape[0] - block_len
    far_ref[...] = jnp.concatenate(halves(table_ref[period:body, :].T[:used]), axis=0)
    here_ref[...] = jnp.concatenate(halves(table_ref[body:, :].T[:used]), axis=0)
    place = lax.broadcasted_iota(jnp.int32, (period, LANES), 0)
    weight = jnp.where(lax.rem(place, block_len) == 0, 1.0 / period, 2.0 / period)
    spec_t = (spec * weight).T
    grad_rows = jnp.concatenate([spec_t[:modes], spec_t[2 * modes : 3 * modes]], axis=0)
    near_ref[...] = jnp.concatenate(halves(grad_rows), axis=0)


def main_kernel(modes, blocks, block_len, taps, channels, table_ref, short_ref, res_ref, fwd_ref, far_ref, here_ref,
                near_ref, grad_ref, mate_ref, *refs):
    bits = blocks.bit_length() - 1
    ids_refs, refs = refs[: bits + 1], refs[bits + 1 :]
    part_ref, query_ref, gated_ref, spec_ref, state_ref, onehot, ids = refs
    half = channels // 2
    groups = half // GROUP
    first = half_index() * half
    filled = 0
    for ref in ids_refs:
        ids[filled : filled + ref.shape[0], :] = ref[...]
        filled += ref.shape[0]
    seq_len = blocks * block_len
    vocab = table_ref.shape[1]
    own = lax.axis_index("ctx")
    order_one = order_matrix(block_len)
    order = jnp.concatenate([order_one * 16, order_one], axis=1)
    on_hi = (own & 1) == 1
    lane = lax.broadcasted_iota(jnp.int32, (block_len, LANES), 1).astype(F32)
    for place in range(blocks):
        source = lax.rem((own & -2) + 2 + place, blocks)
        flags = [((source ^ own) >> bit) & 1 for bit in range(bits)]
        slot = sum(flag << (bits - 1 - bit) for bit, flag in enumerate(flags) if bit > 0)
        slot = slot | (functools.reduce(lambda a, b: a ^ b, flags) << (bits - 1))
        row = ids[pl.ds(slot, 1), :]
        digits = jnp.concatenate([row >> 4, row & 15], axis=1).astype(F32)
        digits = jnp.broadcast_to(digits, (LANES, 2 * block_len)).astype(BF16)
        column = lax.dot_general(order, digits, (((1,), (1,)), ((), ())), preferred_element_type=F32)
        for piece in range(vocab // LANES):
            onehot[pl.ds(place * block_len, block_len), pl.ds(piece * LANES, LANES)] = jnp.where(
                column == lane + float(piece * LANES), 1.0, 0.0
            ).astype(BF16)
    body = seq_len - block_len
    period = 2 * block_len
    halo = SUBLANES * (taps - 1)
    rate = jnp.zeros((modes, 1), F32)
    last = lax.broadcasted_iota(jnp.int32, (halo, GROUP), 0) % SUBLANES == SUBLANES - 1

    def gather(group, part, rows):
        block = table_ref[pl.ds(pl.multiple_of(first + part * channels + group * GROUP, GROUP), GROUP), :]
        return lax.dot_general(onehot[rows:, :], block, (((1,), (1,)), ((), ())), preferred_element_type=F32)

    def features(group):
        return gather(group, 0, body - block_len - halo), gather(group, 1, 0), gather(group, 2, 0)

    def short_conv(feat, at, weights):
        tail = feat[(at - halo) % feat.shape[0] :][:halo]
        block = feat[at : at + block_len]
        ahead = jnp.where(last, tail, block[block_len - halo :]).reshape(taps - 1, SUBLANES, GROUP)
        ahead = pltpu.roll(ahead, 1, 1).reshape(halo, GROUP)
        padded = jnp.concatenate([ahead, block], axis=0)
        total = None
        for tap in range(taps):
            term = weights[tap : tap + 1] * padded[tap * SUBLANES : tap * SUBLANES + block_len]
            total = term if total is None else total + term
        return total

    def one_group(group, feats, rate):
        weights = [
            short_ref[:, pl.ds(pl.multiple_of(first + part * channels + group * GROUP, GROUP), GROUP)]
            for part in range(3)
        ]
        query = [short_conv(feats[0], halo + at, weights[0]) for at in (0, block_len)]
        query = jnp.concatenate(query, axis=1)
        gated = []
        for place in range(blocks):
            keys, vals = (short_conv(feats[part], place * block_len, weights[part]) for part in (1, 2))
            gated.append((keys * vals).astype(BF16))
        ahead_lo = jnp.concatenate([gated[-1], *gated[:-2]], axis=0)
        gated_far = jnp.concatenate([ahead_lo, jnp.concatenate(gated[:-1], axis=0)], axis=1)
        gated_own = jnp.concatenate(gated[-2:], axis=1)
        span = pl.ds(group * WIDE, WIDE)
        query_ref[:, span] = query
        gated_ref[:, span] = gated_own
        rows = pl.ds(group * GROUP, GROUP)
        own_grad, mate_grad = grad_ref[rows, :], mate_ref[rows, :]
        grads = jnp.concatenate(
            [jnp.where(on_hi, mate_grad, own_grad), jnp.where(on_hi, own_grad, mate_grad)], axis=0
        )
        grads = lax.dot_general(order_one, grads, (((1,), (1,)), ((), ())), preferred_element_type=F32)
        dconv = query * grads
        dconv_both = jnp.concatenate(halves(dconv), axis=0)
        spec = dot(fwd_ref[...], gated_own)
        spec = spec[:period] + spec[period:]
        spec_ref[:, span] = spec
        left = jnp.concatenate([fwd_ref[...], here_ref[...]], axis=0)
        dspec = dot(jnp.concatenate([left, left], axis=1), dconv_both)
        dstate = dspec[2 * period :]
        dspec = dspec[:period] + dspec[period : 2 * period]
        dstate = dstate[: 4 * modes] + dstate[4 * modes :]
        state = dot(far_ref[...], gated_far)
        state = state[: 4 * modes] + state[4 * modes :]
        left_re, left_im = spec[:block_len], spec[block_len:]
        right_re, right_im = dspec[:block_len], dspec[block_len:]
        leading = lax.broadcasted_iota(jnp.int32, (block_len, WIDE), 0) == 0
        rere, imim = left_re * right_re, left_im * right_im
        cross_re = jnp.where(leading, rere, rere + imim)
        cross_im = jnp.where(leading, imim, left_re * right_im - left_im * right_re)
        cross = jnp.concatenate([cross_re, cross_im], axis=0)
        cross_hi, cross_lo = halves(cross)
        near = near_ref[...]
        terms = dot(near, cross_hi) + dot(near, cross_lo)
        terms = terms[: 2 * modes] + terms[2 * modes :]
        sc, ss, sc1, ss1 = (state[i * modes : (i + 1) * modes] for i in range(4))
        dc, ds, dc1, ds1 = (dstate[i * modes : (i + 1) * modes] for i in range(4))
        grad = terms[:modes] + dc * sc - ds * ss
        slope = terms[modes:] + dc1 * sc + dc * sc1 - ds1 * ss - ds * ss1
        res = res_ref[:, pl.ds(pl.multiple_of(first + group * GROUP, GROUP), GROUP)]
        both = jnp.concatenate([res, res], axis=1)
        state_ref[:modes, span] = both * sc
        state_ref[modes:, span] = -(both * ss)
        grad = grad[:, :GROUP] + grad[:, GROUP:]
        slope = slope[:, :GROUP] + slope[:, GROUP:]
        for side in range(GROUP // LANES):
            at = (group * GROUP + side * LANES) // LANES * modes
            part_ref[pl.ds(at, modes), :] = grad[:, side * LANES : (side + 1) * LANES]
        return rate + jnp.sum(res * slope, axis=1, keepdims=True)

    feats = features(0)
    for group in range(groups):
        ahead = features(group + 1) if group + 1 < groups else None
        rate = one_group(group, feats, rate)
        feats = ahead
    wide = jnp.broadcast_to(rate, (modes, LANES))
    square = jnp.concatenate([wide, jnp.zeros((LANES - modes, LANES), F32)], axis=0).T
    part_ref[pl.ds(half // LANES * modes, SUBLANES), :] = square[:SUBLANES]


def filter_kernel(modes, block_len, spec_ref, table_ref, res_ref, inv_ref, skip_ref, filt_ref, inv_out, skip_out, inv, copied):
    copies = [
        pltpu.make_async_copy(inv_ref, inv, copied.at[0]),
        pltpu.make_async_copy(skip_ref, skip_out, copied.at[1]),
    ]
    for copy in copies:
        copy.start()
    period = 2 * block_len
    spec_hi, spec_lo = halves(spec_ref[:, :modes])
    half = res_ref.shape[1] // 2
    res_hi, res_lo = halves(res_ref[:, pl.ds(pl.multiple_of(half_index() * half, half), half)])
    left = jnp.concatenate([spec_hi, spec_hi, spec_lo], axis=1)
    filt_ref[...] = dot(left, jnp.concatenate([res_hi, res_lo, res_hi], axis=0))
    for copy in copies:
        copy.wait()
    here = table_ref[table_ref.shape[0] - block_len :, : 2 * modes]
    inv_hi, inv_lo = halves(jnp.concatenate([inv[...], here], axis=1))
    inv_out[...] = jnp.concatenate([inv_hi, inv_lo], axis=0)


def mixed_kernel(block_len, query_ref, gated_ref, spec_ref, filt_ref, state_ref, inv_ref, skip_ref, own_ref, mate_ref):
    half = filt_ref.shape[1]
    first = half_index() * half
    on_hi = (lax.axis_index("ctx") & 1) == 1
    leading = lax.broadcasted_iota(jnp.int32, (block_len, WIDE), 0) == 0
    order = order_matrix(block_len, True)
    inv = inv_ref[...]
    for group in range(half // GROUP):
        span = pl.ds(group * WIDE, WIDE)
        rows = pl.ds(group * GROUP, GROUP)
        filt = filt_ref[:, rows]
        filt = jnp.concatenate([filt, filt], axis=1)
        skip = skip_ref[:, pl.ds(pl.multiple_of(first + group * GROUP, GROUP), GROUP)]
        left_re, left_im = filt[:block_len], filt[block_len:]
        right_re, right_im = spec_ref[:block_len, span], spec_ref[block_len:, span]
        rere, imim = left_re * right_re, left_im * right_im
        out_re = jnp.where(leading, rere, rere - imim)
        out_im = jnp.where(leading, imim, left_re * right_im + left_im * right_re)
        spec_hi, spec_lo = halves(jnp.concatenate([out_re, out_im, state_ref[:, span]], axis=0))
        conv = dot(inv, spec_hi)
        conv = conv[:block_len] + conv[block_len:] + dot(inv[:block_len], spec_lo)
        through = jnp.concatenate([skip, skip], axis=1) * gated_ref[:, span].astype(F32)
        mixed = dot(order, (query_ref[:, span] * (conv + through)).astype(BF16))
        low, high = mixed[:, :GROUP], mixed[:, GROUP:]
        own_ref[rows, :] = jnp.where(on_hi, high, low).T.astype(BF16)
        mate_ref[rows, :] = jnp.where(on_hi, low, high).T.astype(BF16)


def call(kernel, outs, scratch, args, cost, spaces=None, out_spaces=None):
    return pl.pallas_call(
        kernel,
        out_shape=[jax.ShapeDtypeStruct(shape, dtype) for shape, dtype in outs],
        in_specs=[pl.BlockSpec(memory_space=space) for space in spaces or [pltpu.VMEM] * len(args)],
        out_specs=[pl.BlockSpec(memory_space=space) for space in out_spaces or [pltpu.VMEM] * len(outs)],
        scratch_shapes=scratch,
        compiler_params=pltpu.CompilerParams(vmem_limit_bytes=40 * 1024 * 1024),
        cost_estimate=pl.CostEstimate(flops=cost[0], bytes_accessed=cost[1], transcendentals=0),
    )(*args)


def output_kernel(own_ref, mate_ref, mixed_ref, copied):
    half = own_ref.shape[0]
    second = half_index()
    copies = []
    for at, (source, place) in enumerate(((own_ref, second), (mate_ref, 1 - second))):
        target = mixed_ref.at[pl.ds(pl.multiple_of(place * half, half), half)]
        copies.append(pltpu.make_async_copy(source, target, copied.at[at]))
    for copy in copies:
        copy.start()
    for copy in copies:
        copy.wait()


def result_kernel(modes, part_ref, moved_ref, grad_ref, rate_ref):
    half = grad_ref.shape[1] // 2
    second = half_index()
    for tile in range(half // LANES):
        rows = pl.ds(tile * modes, modes)
        part, moved = part_ref[rows, :], moved_ref[rows, :]
        grad_ref[:, pl.ds(tile * LANES, LANES)] = jnp.where(second == 1, moved, part)
        grad_ref[:, pl.ds(half + tile * LANES, LANES)] = jnp.where(second == 1, part, moved)
    last = half // LANES * modes
    rate_ref[...] = (part_ref[last : last + 1, :] + moved_ref[last : last + 1, :])[:, :modes]


def per_device(token_ids, feature_table, short_weight, residue, rates, skip_gain, grad_out):
    block_len = token_ids.shape[1]
    blocks = lax.axis_size("ctx")
    seq_len = block_len * blocks
    channels, modes = residue.shape
    taps = short_weight.shape[1]
    vocab = feature_table.shape[1]
    period = 2 * block_len
    forward, inverse = dft_tables(block_len)
    wave = mode_constants(block_len, seq_len, modes)
    half = channels // 2

    masks = [mask | 1 for mask in masks_of(blocks)[:0:-1]] + [1]
    moved_ids = [xor_permute(token_ids, ("ctx",), masks[0])]

    def in_hbm(*arrays):
        return [pltpu.with_memory_space_constraint(array, pltpu.HBM) for array in arrays]

    vmem, hbm = pltpu.VMEM, pltpu.HBM
    ids, short, res, forward, table, keep_grad, send_grad = call(
        functools.partial(inputs_kernel, modes, block_len, seq_len),
        [
            ((1, block_len), jnp.int32),
            (short_weight.shape[::-1], F32),
            ((modes, channels), F32),
            (forward.shape, F32),
            (wave.shape, F32),
            ((half, block_len), BF16),
            ((half, block_len), BF16),
        ],
        [
            vmem((1, modes), F32),
            vmem((1, LANES), F32),
            vmem(wave.shape, F32),
            pltpu.SemaphoreType.DMA((8,)),
        ],
        in_hbm(
            rates[None],
            jnp.asarray(wave),
            jnp.asarray(forward.astype(np.float32)),
            token_ids,
            residue.T,
            short_weight.T,
            grad_out[0],
        ),
        (10_000_000_000, 40_000_000),
        [hbm] * 7,
    )
    mate_grad = xor_permute(send_grad, ("ctx",), 1)
    for mask in masks[1:]:
        known = jnp.concatenate([ids, *moved_ids], axis=0)
        if mask == masks[-1]:
            known, table = lax.optimization_barrier((known, table))
        moved_ids.append(xor_permute(known, ("ctx",), mask))
    fwd, far, here, near, table_spec = call(
        functools.partial(tables_kernel, modes, block_len),
        [
            ((2 * period, block_len), BF16),
            ((8 * modes, seq_len - block_len), BF16),
            ((8 * modes, block_len), BF16),
            ((4 * modes, period), BF16),
            ((period, LANES), F32),
        ],
        [],
        [table, forward],
        (300_000_000, 1_000_000),
    )
    part, query, gated, spec, state = call(
        functools.partial(main_kernel, modes, blocks, block_len, taps, channels),
        [
            ((half // LANES * modes + SUBLANES, LANES), F32),
            ((block_len, channels), F32),
            ((block_len, channels), BF16),
            ((period, channels), F32),
            ((2 * modes, channels), F32),
        ],
        [
            vmem((seq_len, vocab), BF16),
            vmem((blocks, block_len), jnp.int32),
        ],
        [feature_table, short, res, fwd, far, here, near, keep_grad, mate_grad, ids, *moved_ids],
        (4 * seq_len * vocab * channels, 6_000_000),
    )
    core = lax.axis_size("dp")
    hops = [mask | core for mask in masks_of(blocks * core) if mask != core]
    for hop in hops:
        if hop == hops[0]:
            part, res = lax.optimization_barrier((part, res))
            filt, inv, skip = call(
                functools.partial(filter_kernel, modes, block_len),
                [((period, half), F32), ((2 * block_len, period + 2 * modes), BF16), ((1, channels), F32)],
                [vmem(inverse.shape, F32), pltpu.SemaphoreType.DMA((2,))],
                [table_spec, table, res, *in_hbm(jnp.asarray(inverse.astype(np.float32)), skip_gain[None])],
                (50_000_000, 1_500_000),
                [vmem, vmem, vmem, hbm, hbm],
            )
        if hop == hops[1]:
            part, query, filt = lax.optimization_barrier((part, query, filt))
            mixed_own, mixed_mate = call(
                functools.partial(mixed_kernel, block_len),
                [((half, block_len), BF16)] * 2,
                [],
                [query, gated, spec, filt, state, inv, skip],
                (300_000_000, 3_000_000),
            )
        if hop == hops[2]:
            part, mixed_mate = lax.optimization_barrier((part, mixed_mate))
            mixed_moved = xor_permute(mixed_mate, ("ctx", "dp"), core)
        if hop == hops[3]:
            part, mixed_moved = lax.optimization_barrier((part, mixed_moved))
            (mixed,) = call(
                output_kernel,
                [((channels, block_len), BF16)],
                [pltpu.SemaphoreType.DMA((2,))],
                [mixed_own, mixed_moved],
                (0, 800_000),
                out_spaces=[hbm],
            )
        part = part + xor_permute(part, ("ctx", "dp"), hop)
    part, mixed = lax.optimization_barrier((part, mixed))
    grad, rate = call(
        functools.partial(result_kernel, modes),
        [((modes, channels), F32), ((1, modes), F32)],
        [],
        [part, xor_permute(part, ("ctx", "dp"), core)],
        (0, 200_000),
    )
    return (mixed[None], grad.T, rate[0])


def solution(mesh):
    return jax.shard_map(
        per_device,
        mesh=mesh,
        in_specs=(P("dp", "ctx"), P(), P(), P(), P(), P(), P("dp", None, "ctx")),
        out_specs=(P("dp", None, "ctx"), P(), P()),
        check_vma=False,
    )
```

```python
import functools
import math

import jax
import jax.numpy as jnp
import numpy as np
from jax import lax
from jax.experimental import pallas as pl
from jax.experimental.pallas import tpu as pltpu
from jax.sharding import PartitionSpec as P

F32 = jnp.float32
BF16 = jnp.bfloat16
GROUP = 256
WIDE = 2 * GROUP
SUBLANES = 8
LANES = 128


def xor_permute(block, axis, mask):
    size = math.prod(lax.axis_size(name) for name in axis)
    return lax.ppermute(block, axis, [(i, i ^ mask) for i in range(size)])


def masks_of(size):
    return [1 << bit for bit in range(size.bit_length() - 1)]


def half_index():
    bits = lax.axis_index("ctx") ^ lax.axis_index("dp")
    for shift in (4, 2, 1):
        bits = bits ^ (bits >> shift)
    return bits & 1


def halves(table):
    upper = table.astype(BF16)
    return upper, (table - upper.astype(F32)).astype(BF16)


def dot(left, right):
    return jnp.dot(left, right, preferred_element_type=F32)


def row_token(row, block_len):
    return row % SUBLANES * (block_len // SUBLANES) + row // SUBLANES


def order_matrix(block_len, transposed=False):
    row = lax.broadcasted_iota(jnp.int32, (block_len, block_len), 1 if transposed else 0)
    token = lax.broadcasted_iota(jnp.int32, (block_len, block_len), 0 if transposed else 1)
    return jnp.where(row_token(row, block_len) == token, 1.0, 0.0).astype(BF16)


def dft_tables(block_len):
    period = 2 * block_len
    column = np.arange(block_len)[:, None]
    row = np.arange(block_len)
    sample = np.concatenate([row_token(row, block_len), block_len + row_token(row, block_len)])[None, :]
    angle = (column * sample % period) * (2.0 * math.pi / period)
    parity = 1.0 - 2.0 * (sample % 2)
    imag = np.where(column == 0, parity, -np.sin(angle))
    forward = np.concatenate([np.cos(angle), imag], axis=0)
    weight = np.where(np.arange(period) % block_len == 0, 1.0, 2.0) / period
    inverse = (forward[:, :block_len] * weight[:, None]).T
    return forward, inverse


def row_delays(block_len, seq_len, row):
    token = row_token(row % block_len, block_len) + row // block_len * block_len
    period = 2 * block_len
    body = seq_len - block_len

    def near(n):
        return n + (n >= block_len) * (seq_len - period)

    return near, lambda n: body - n, lambda n: n, token


def mode_constants(block_len, seq_len, modes):
    parts = []
    for at, length in enumerate((2 * block_len, seq_len - block_len, block_len)):
        delays = row_delays(block_len, seq_len, np.arange(length))
        parts.append(delays[at](delays[3]))
    delay = np.concatenate(parts)[:, None]
    period = 2 * modes + 2
    angle = (delay * (np.arange(modes)[None, :] + 1) % period) * (2.0 * math.pi / period)
    ratio = delay / seq_len
    parts = [np.cos(angle), np.sin(angle), -ratio * np.cos(angle), -ratio * np.sin(angle)]
    wave = np.concatenate(parts, axis=1)
    return np.pad(wave, ((0, 0), (0, LANES - wave.shape[1]))).astype(np.float32)


def inputs_kernel(modes, block_len, seq_len, *refs):
    sources, outs, scratch = refs[:7], refs[7:14], refs[14:]
    ids_out, short_out, res_out, fwd_out, table_ref, keep_ref, send_ref = outs
    few, rate_row, wave, copied = scratch
    half = keep_ref.shape[0]
    second = half_index()
    grads = [sources[6].at[pl.ds(pl.multiple_of(place * half, half), half)] for place in (1 - second, second)]
    targets = [few, wave, send_ref, fwd_out, ids_out, res_out, short_out, keep_ref]
    pairs = zip([*sources[:2], grads[0], *sources[2:6], grads[1]], targets, strict=True)
    copies = [pltpu.make_async_copy(*pair, copied.at[i]) for i, pair in enumerate(pairs)]
    for copy in copies:
        copy.start()
    rate_row[...] = jnp.zeros_like(rate_row)
    copies[0].wait()
    rate_row[:, :modes] = few[...]
    rates = rate_row[...]
    for shift in (modes, 2 * modes):
        rates = rates + pltpu.roll(rates, shift, 1)
    start = 0
    decays = []
    for at, length in enumerate((2 * block_len, seq_len - block_len, block_len)):
        delays = row_delays(block_len, seq_len, lax.broadcasted_iota(jnp.int32, (length, LANES), 0))
        decays.append(jnp.exp(delays[at](delays[3]).astype(F32) * (-1.0 / seq_len) * rates))
    copies[1].wait()
    for decay in decays:
        rows = pl.ds(start, decay.shape[0])
        table_ref[rows, :] = decay * wave[rows, :]
        start += decay.shape[0]
    for copy in copies[2:]:
        copy.wait()


def tables_kernel(modes, block_len, table_ref, fwd_ref, fwd_out, far_ref, here_ref, near_ref, spec_ref):
    period = 2 * block_len
    used = 4 * modes
    near_hi, near_lo = halves(table_ref[:period, :])
    fwd_hi, fwd_lo = halves(fwd_ref[...])
    spec = dot(fwd_hi, near_hi) + dot(fwd_hi, near_lo) + dot(fwd_lo, near_hi)
    fwd_out[:period, :] = fwd_hi[:, :block_len]
    fwd_out[period:, :] = fwd_lo[:, :block_len]
    spec_ref[...] = spec
    body = table_ref.shape[0] - block_len
    far_ref[...] = jnp.concatenate(halves(table_ref[period:body, :].T[:used]), axis=0)
    here_ref[...] = jnp.concatenate(halves(table_ref[body:, :].T[:used]), axis=0)
    place = lax.broadcasted_iota(jnp.int32, (period, LANES), 0)
    weight = jnp.where(lax.rem(place, block_len) == 0, 1.0 / period, 2.0 / period)
    spec_t = (spec * weight).T
    grad_rows = jnp.concatenate([spec_t[:modes], spec_t[2 * modes : 3 * modes]], axis=0)
    near_ref[...] = jnp.concatenate(halves(grad_rows), axis=0)


def main_kernel(modes, blocks, block_len, taps, channels, table_ref, short_ref, res_ref, fwd_ref, far_ref, here_ref,
                near_ref, grad_ref, mate_ref, *refs):
    bits = blocks.bit_length() - 1
    ids_refs, refs = refs[: bits + 1], refs[bits + 1 :]
    part_ref, query_ref, gated_ref, spec_ref, state_ref, onehot, ids = refs
    half = channels // 2
    groups = half // GROUP
    first = half_index() * half
    filled = 0
    for ref in ids_refs:
        ids[filled : filled + ref.shape[0], :] = ref[...]
        filled += ref.shape[0]
    seq_len = blocks * block_len
    vocab = table_ref.shape[1]
    own = lax.axis_index("ctx")
    order_one = order_matrix(block_len)
    order = jnp.concatenate([order_one * 16, order_one], axis=1)
    on_hi = (own & 1) == 1
    lane = lax.broadcasted_iota(jnp.int32, (block_len, LANES), 1).astype(F32)
    for place in range(blocks):
        source = lax.rem((own & -2) + 2 + place, blocks)
        flags = [((source ^ own) >> bit) & 1 for bit in range(bits)]
        slot = sum(flag << (bits - 1 - bit) for bit, flag in enumerate(flags) if bit > 0)
        slot = slot | (functools.reduce(lambda a, b: a ^ b, flags) << (bits - 1))
        row = ids[pl.ds(slot, 1), :]
        digits = jnp.concatenate([row >> 4, row & 15], axis=1).astype(F32)
        digits = jnp.broadcast_to(digits, (LANES, 2 * block_len)).astype(BF16)
        column = lax.dot_general(order, digits, (((1,), (1,)), ((), ())), preferred_element_type=F32)
        for piece in range(vocab // LANES):
            onehot[pl.ds(place * block_len, block_len), pl.ds(piece * LANES, LANES)] = jnp.where(
                column == lane + float(piece * LANES), 1.0, 0.0
            ).astype(BF16)
    body = seq_len - block_len
    period = 2 * block_len
    halo = SUBLANES * (taps - 1)
    rate = jnp.zeros((modes, 1), F32)
    last = lax.broadcasted_iota(jnp.int32, (halo, GROUP), 0) % SUBLANES == SUBLANES - 1

    def gather(group, part, rows):
        block = table_ref[pl.ds(pl.multiple_of(first + part * channels + group * GROUP, GROUP), GROUP), :]
        return lax.dot_general(onehot[rows:, :], block, (((1,), (1,)), ((), ())), preferred_element_type=F32)

    def features(group):
        return gather(group, 0, body - block_len - halo), gather(group, 1, 0), gather(group, 2, 0)

    def short_conv(feat, at, weights):
        tail = feat[(at - halo) % feat.shape[0] :][:halo]
        block = feat[at : at + block_len]
        ahead = jnp.where(last, tail, block[block_len - halo :]).reshape(taps - 1, SUBLANES, GROUP)
        ahead = pltpu.roll(ahead, 1, 1).reshape(halo, GROUP)
        padded = jnp.concatenate([ahead, block], axis=0)
        total = None
        for tap in range(taps):
            term = weights[tap : tap + 1] * padded[tap * SUBLANES : tap * SUBLANES + block_len]
            total = term if total is None else total + term
        return total

    def one_group(group, feats, rate):
        weights = [
            short_ref[:, pl.ds(pl.multiple_of(first + part * channels + group * GROUP, GROUP), GROUP)]
            for part in range(3)
        ]
        query = [short_conv(feats[0], halo + at, weights[0]) for at in (0, block_len)]
        query = jnp.concatenate(query, axis=1)
        gated = []
        for place in range(blocks):
            keys, vals = (short_conv(feats[part], place * block_len, weights[part]) for part in (1, 2))
            gated.append((keys * vals).astype(BF16))
        ahead_lo = jnp.concatenate([gated[-1], *gated[:-2]], axis=0)
        gated_far = jnp.concatenate([ahead_lo, jnp.concatenate(gated[:-1], axis=0)], axis=1)
        gated_own = jnp.concatenate(gated[-2:], axis=1)
        span = pl.ds(group * WIDE, WIDE)
        query_ref[:, span] = query
        gated_ref[:, span] = gated_own
        rows = pl.ds(group * GROUP, GROUP)
        own_grad, mate_grad = grad_ref[rows, :], mate_ref[rows, :]
        grads = jnp.concatenate(
            [jnp.where(on_hi, mate_grad, own_grad), jnp.where(on_hi, own_grad, mate_grad)], axis=0
        )
        grads = lax.dot_general(order_one, grads, (((1,), (1,)), ((), ())), preferred_element_type=F32)
        dconv = query * grads
        dconv_both = jnp.concatenate(halves(dconv), axis=0)
        spec = dot(fwd_ref[...], gated_own)
        spec = spec[:period] + spec[period:]
        spec_ref[:, span] = spec
        left = jnp.concatenate([fwd_ref[...], here_ref[...]], axis=0)
        dspec = dot(jnp.concatenate([left, left], axis=1), dconv_both)
        dstate = dspec[2 * period :]
        dspec = dspec[:period] + dspec[period : 2 * period]
        dstate = dstate[: 4 * modes] + dstate[4 * modes :]
        state = dot(far_ref[...], gated_far)
        state = state[: 4 * modes] + state[4 * modes :]
        left_re, left_im = spec[:block_len], spec[block_len:]
        right_re, right_im = dspec[:block_len], dspec[block_len:]
        leading = lax.broadcasted_iota(jnp.int32, (block_len, WIDE), 0) == 0
        rere, imim = left_re * right_re, left_im * right_im
        cross_re = jnp.where(leading, rere, rere + imim)
        cross_im = jnp.where(leading, imim, left_re * right_im - left_im * right_re)
        cross = jnp.concatenate([cross_re, cross_im], axis=0)
        cross_hi, cross_lo = halves(cross)
        near = near_ref[...]
        terms = dot(near, cross_hi) + dot(near, cross_lo)
        terms = terms[: 2 * modes] + terms[2 * modes :]
        sc, ss, sc1, ss1 = (state[i * modes : (i + 1) * modes] for i in range(4))
        dc, ds, dc1, ds1 = (dstate[i * modes : (i + 1) * modes] for i in range(4))
        grad = terms[:modes] + dc * sc - ds * ss
        slope = terms[modes:] + dc1 * sc + dc * sc1 - ds1 * ss - ds * ss1
        res = res_ref[:, pl.ds(pl.multiple_of(first + group * GROUP, GROUP), GROUP)]
        both = jnp.concatenate([res, res], axis=1)
        state_ref[:modes, span] = both * sc
        state_ref[modes:, span] = -(both * ss)
        grad = grad[:, :GROUP] + grad[:, GROUP:]
        slope = slope[:, :GROUP] + slope[:, GROUP:]
        for side in range(GROUP // LANES):
            at = (group * GROUP + side * LANES) // LANES * modes
            part_ref[pl.ds(at, modes), :] = grad[:, side * LANES : (side + 1) * LANES]
        return rate + jnp.sum(res * slope, axis=1, keepdims=True)

    feats = features(0)
    for group in range(groups):
        ahead = features(group + 1) if group + 1 < groups else None
        rate = one_group(group, feats, rate)
        feats = ahead
    wide = jnp.broadcast_to(rate, (modes, LANES))
    square = jnp.concatenate([wide, jnp.zeros((LANES - modes, LANES), F32)], axis=0).T
    part_ref[pl.ds(half // LANES * modes, SUBLANES), :] = square[:SUBLANES]


def filter_kernel(modes, block_len, spec_ref, table_ref, res_ref, inv_ref, skip_ref, filt_ref, inv_out, skip_out, inv, copied):
    copies = [
        pltpu.make_async_copy(inv_ref, inv, copied.at[0]),
        pltpu.make_async_copy(skip_ref, skip_out, copied.at[1]),
    ]
    for copy in copies:
        copy.start()
    period = 2 * block_len
    spec_hi, spec_lo = halves(spec_ref[:, :modes])
    half = res_ref.shape[1] // 2
    res_hi, res_lo = halves(res_ref[:, pl.ds(pl.multiple_of(half_index() * half, half), half)])
    left = jnp.concatenate([spec_hi, spec_hi, spec_lo], axis=1)
    filt_ref[...] = dot(left, jnp.concatenate([res_hi, res_lo, res_hi], axis=0))
    for copy in copies:
        copy.wait()
    here = table_ref[table_ref.shape[0] - block_len :, : 2 * modes]
    inv_hi, inv_lo = halves(jnp.concatenate([inv[...], here], axis=1))
    inv_out[...] = jnp.concatenate([inv_hi, inv_lo], axis=0)


def mixed_kernel(block_len, query_ref, gated_ref, spec_ref, filt_ref, state_ref, inv_ref, skip_ref, own_ref, mate_ref):
    half = filt_ref.shape[1]
    first = half_index() * half
    on_hi = (lax.axis_index("ctx") & 1) == 1
    leading = lax.broadcasted_iota(jnp.int32, (block_len, WIDE), 0) == 0
    order = order_matrix(block_len, True)
    inv = inv_ref[...]
    for group in range(half // GROUP):
        span = pl.ds(group * WIDE, WIDE)
        rows = pl.ds(group * GROUP, GROUP)
        filt = filt_ref[:, rows]
        filt = jnp.concatenate([filt, filt], axis=1)
        skip = skip_ref[:, pl.ds(pl.multiple_of(first + group * GROUP, GROUP), GROUP)]
        left_re, left_im = filt[:block_len], filt[block_len:]
        right_re, right_im = spec_ref[:block_len, span], spec_ref[block_len:, span]
        rere, imim = left_re * right_re, left_im * right_im
        out_re = jnp.where(leading, rere, rere - imim)
        out_im = jnp.where(leading, imim, left_re * right_im + left_im * right_re)
        spec_hi, spec_lo = halves(jnp.concatenate([out_re, out_im, state_ref[:, span]], axis=0))
        conv = dot(inv, spec_hi)
        conv = conv[:block_len] + conv[block_len:] + dot(inv[:block_len], spec_lo)
        through = jnp.concatenate([skip, skip], axis=1) * gated_ref[:, span].astype(F32)
        mixed = dot(order, (query_ref[:, span] * (conv + through)).astype(BF16))
        low, high = mixed[:, :GROUP], mixed[:, GROUP:]
        own_ref[rows, :] = jnp.where(on_hi, high, low).T.astype(BF16)
        mate_ref[rows, :] = jnp.where(on_hi, low, high).T.astype(BF16)


def call(kernel, outs, scratch, args, cost, spaces=None, out_spaces=None):
    return pl.pallas_call(
        kernel,
        out_shape=[jax.ShapeDtypeStruct(shape, dtype) for shape, dtype in outs],
        in_specs=[pl.BlockSpec(memory_space=space) for space in spaces or [pltpu.VMEM] * len(args)],
        out_specs=[pl.BlockSpec(memory_space=space) for space in out_spaces or [pltpu.VMEM] * len(outs)],
        scratch_shapes=scratch,
        compiler_params=pltpu.CompilerParams(vmem_limit_bytes=40 * 1024 * 1024),
        cost_estimate=pl.CostEstimate(flops=cost[0], bytes_accessed=cost[1], transcendentals=0),
    )(*args)


def output_kernel(own_ref, mate_ref, mixed_ref, copied):
    half = own_ref.shape[0]
    second = half_index()
    copies = []
    for at, (source, place) in enumerate(((own_ref, second), (mate_ref, 1 - second))):
        target = mixed_ref.at[pl.ds(pl.multiple_of(place * half, half), half)]
        copies.append(pltpu.make_async_copy(source, target, copied.at[at]))
    for copy in copies:
        copy.start()
    for copy in copies:
        copy.wait()


def result_kernel(modes, part_ref, moved_ref, grad_ref, rate_ref):
    half = grad_ref.shape[1] // 2
    second = half_index()
    for tile in range(half // LANES):
        rows = pl.ds(tile * modes, modes)
        part, moved = part_ref[rows, :], moved_ref[rows, :]
        grad_ref[:, pl.ds(tile * LANES, LANES)] = jnp.where(second == 1, moved, part)
        grad_ref[:, pl.ds(half + tile * LANES, LANES)] = jnp.where(second == 1, part, moved)
    last = half // LANES * modes
    rate_ref[...] = (part_ref[last : last + 1, :] + moved_ref[last : last + 1, :])[:, :modes]


def rounded(value):
    return lax.reduce_precision(value, 8, 7)


def per_device(token_ids, feature_table, short_weight, residue, rates, skip_gain, grad_out):
    block_len = token_ids.shape[1]
    blocks = lax.axis_size("ctx")
    seq_len = block_len * blocks
    channels, modes = residue.shape
    taps = short_weight.shape[1]
    vocab = feature_table.shape[1]
    period = 2 * block_len
    forward, inverse = dft_tables(block_len)
    wave = mode_constants(block_len, seq_len, modes)
    half = channels // 2

    masks = [mask | 1 for mask in masks_of(blocks)[:0:-1]] + [1]
    moved_ids = [xor_permute(token_ids, ("ctx",), masks[0])]

    def in_hbm(*arrays):
        return [pltpu.with_memory_space_constraint(array, pltpu.HBM) for array in arrays]

    vmem, hbm = pltpu.VMEM, pltpu.HBM
    ids, short, res, forward, table, keep_grad, send_grad = call(
        functools.partial(inputs_kernel, modes, block_len, seq_len),
        [
            ((1, block_len), jnp.int32),
            (short_weight.shape[::-1], F32),
            ((modes, channels), F32),
            (forward.shape, F32),
            (wave.shape, F32),
            ((half, block_len), BF16),
            ((half, block_len), BF16),
        ],
        [
            vmem((1, modes), F32),
            vmem((1, LANES), F32),
            vmem(wave.shape, F32),
            pltpu.SemaphoreType.DMA((8,)),
        ],
        in_hbm(
            rates[None],
            jnp.asarray(wave),
            jnp.asarray(forward.astype(np.float32)),
            token_ids,
            residue.T,
            short_weight.T,
            grad_out[0],
        ),
        (10_000_000_000, 40_000_000),
        [hbm] * 7,
    )
    mate_grad = xor_permute(send_grad, ("ctx",), 1)
    for mask in masks[1:]:
        known = jnp.concatenate([ids, *moved_ids], axis=0)
        if mask == masks[-1]:
            known, table = lax.optimization_barrier((known, table))
        moved_ids.append(xor_permute(known, ("ctx",), mask))
    fwd, far, here, near, table_spec = call(
        functools.partial(tables_kernel, modes, block_len),
        [
            ((2 * period, block_len), BF16),
            ((8 * modes, seq_len - block_len), BF16),
            ((8 * modes, block_len), BF16),
            ((4 * modes, period), BF16),
            ((period, LANES), F32),
        ],
        [],
        [table, forward],
        (300_000_000, 1_000_000),
    )
    part, query, gated, spec, state = call(
        functools.partial(main_kernel, modes, blocks, block_len, taps, channels),
        [
            ((half // LANES * modes + SUBLANES, LANES), F32),
            ((block_len, channels), F32),
            ((block_len, channels), BF16),
            ((period, channels), F32),
            ((2 * modes, channels), F32),
        ],
        [
            vmem((seq_len, vocab), BF16),
            vmem((blocks, block_len), jnp.int32),
        ],
        [feature_table, short, res, fwd, far, here, near, keep_grad, mate_grad, ids, *moved_ids],
        (4 * seq_len * vocab * channels, 6_000_000),
    )
    core = lax.axis_size("dp")
    hops = [mask | core for mask in masks_of(blocks * core) if mask != core]
    rows = half // LANES * modes
    rate = part[rows : rows + 1]
    part = part[:rows]
    filler = jnp.zeros((14, LANES), BF16)
    for hop in hops:
        if hop == hops[0]:
            part, res = lax.optimization_barrier((part, res))
            filt, inv, skip = call(
                functools.partial(filter_kernel, modes, block_len),
                [((period, half), F32), ((2 * block_len, period + 2 * modes), BF16), ((1, channels), F32)],
                [vmem(inverse.shape, F32), pltpu.SemaphoreType.DMA((2,))],
                [table_spec, table, res, *in_hbm(jnp.asarray(inverse.astype(np.float32)), skip_gain[None])],
                (50_000_000, 1_500_000),
                [vmem, vmem, vmem, hbm, hbm],
            )
        if hop == hops[1]:
            part, query, filt = lax.optimization_barrier((part, query, filt))
            mixed_own, mixed_mate = call(
                functools.partial(mixed_kernel, block_len),
                [((half, block_len), BF16)] * 2,
                [],
                [query, gated, spec, filt, state, inv, skip],
                (300_000_000, 3_000_000),
            )
        if hop == hops[2]:
            part, mixed_mate = lax.optimization_barrier((part, mixed_mate))
            mixed_moved = xor_permute(mixed_mate, ("ctx", "dp"), core)
        if hop == hops[3]:
            part, mixed_moved = lax.optimization_barrier((part, mixed_moved))
            (mixed,) = call(
                output_kernel,
                [((channels, block_len), BF16)],
                [pltpu.SemaphoreType.DMA((2,))],
                [mixed_own, mixed_moved],
                (0, 800_000),
                out_spaces=[hbm],
            )
        part, upper = rounded(part), rounded(rate)
        lower = rounded(rate - upper)
        sent = jnp.concatenate([part.astype(BF16), upper.astype(BF16), lower.astype(BF16), filler], axis=0)
        moved = xor_permute(sent, ("ctx", "dp"), hop).astype(F32)
        part = part + moved[:rows]
        rate = upper + lower + (moved[rows : rows + 1] + moved[rows + 1 : rows + 2])
    part = jnp.concatenate([part, rate, jnp.zeros((SUBLANES - 1, LANES), F32)], axis=0)
    part, mixed = lax.optimization_barrier((part, mixed))
    grad, rate = call(
        functools.partial(result_kernel, modes),
        [((modes, channels), F32), ((1, modes), F32)],
        [],
        [part, xor_permute(part, ("ctx", "dp"), core)],
        (0, 200_000),
    )
    return (mixed[None], grad.T, rate[0])


def solution(mesh):
    return jax.shard_map(
        per_device,
        mesh=mesh,
        in_specs=(P("dp", "ctx"), P(), P(), P(), P(), P(), P("dp", None, "ctx")),
        out_specs=(P("dp", None, "ctx"), P(), P()),
        check_vma=False,
    )
```

```python
import functools
import math

import jax
import jax.numpy as jnp
import numpy as np
from jax import lax
from jax.experimental import pallas as pl
from jax.experimental.pallas import tpu as pltpu
from jax.sharding import PartitionSpec as P

F32 = jnp.float32
BF16 = jnp.bfloat16
GROUP = 256
WIDE = 2 * GROUP
SUBLANES = 8
LANES = 128


def xor_permute(block, axis, mask):
    size = math.prod(lax.axis_size(name) for name in axis)
    return lax.ppermute(block, axis, [(i, i ^ mask) for i in range(size)])


def masks_of(size):
    return [1 << bit for bit in range(size.bit_length() - 1)]


def half_index():
    bits = lax.axis_index("ctx") ^ lax.axis_index("dp")
    for shift in (4, 2, 1):
        bits = bits ^ (bits >> shift)
    return bits & 1


def halves(table):
    upper = table.astype(BF16)
    return upper, (table - upper.astype(F32)).astype(BF16)


def dot(left, right):
    return jnp.dot(left, right, preferred_element_type=F32)


def row_token(row, block_len):
    return row % SUBLANES * (block_len // SUBLANES) + row // SUBLANES


def order_matrix(block_len, transposed=False):
    row = lax.broadcasted_iota(jnp.int32, (block_len, block_len), 1 if transposed else 0)
    token = lax.broadcasted_iota(jnp.int32, (block_len, block_len), 0 if transposed else 1)
    return jnp.where(row_token(row, block_len) == token, 1.0, 0.0).astype(BF16)


def dft_tables(block_len):
    period = 2 * block_len
    column = np.arange(block_len)[:, None]
    row = np.arange(block_len)
    sample = np.concatenate([row_token(row, block_len), block_len + row_token(row, block_len)])[None, :]
    angle = (column * sample % period) * (2.0 * math.pi / period)
    parity = 1.0 - 2.0 * (sample % 2)
    imag = np.where(column == 0, parity, -np.sin(angle))
    forward = np.concatenate([np.cos(angle), imag], axis=0)
    weight = np.where(np.arange(period) % block_len == 0, 1.0, 2.0) / period
    inverse = (forward[:, :block_len] * weight[:, None]).T
    return forward, inverse


def row_delays(block_len, seq_len, row):
    token = row_token(row % block_len, block_len) + row // block_len * block_len
    period = 2 * block_len
    body = seq_len - block_len

    def near(n):
        return n + (n >= block_len) * (seq_len - period)

    return near, lambda n: body - n, lambda n: n, token


def mode_constants(block_len, seq_len, modes):
    parts = []
    for at, length in enumerate((2 * block_len, seq_len - block_len, block_len)):
        delays = row_delays(block_len, seq_len, np.arange(length))
        parts.append(delays[at](delays[3]))
    delay = np.concatenate(parts)[:, None]
    period = 2 * modes + 2
    angle = (delay * (np.arange(modes)[None, :] + 1) % period) * (2.0 * math.pi / period)
    ratio = delay / seq_len
    parts = [np.cos(angle), np.sin(angle), -ratio * np.cos(angle), -ratio * np.sin(angle)]
    wave = np.concatenate(parts, axis=1)
    return np.pad(wave, ((0, 0), (0, LANES - wave.shape[1]))).astype(np.float32)


def inputs_kernel(modes, block_len, seq_len, *refs):
    sources, outs, scratch = refs[:7], refs[7:14], refs[14:]
    ids_out, short_out, res_out, fwd_out, table_ref, keep_ref, send_ref = outs
    few, rate_row, wave, copied = scratch
    half = keep_ref.shape[0]
    second = half_index()
    grads = [sources[6].at[pl.ds(pl.multiple_of(place * half, half), half)] for place in (1 - second, second)]
    targets = [few, wave, send_ref, fwd_out, ids_out, res_out, short_out, keep_ref]
    pairs = zip([*sources[:2], grads[0], *sources[2:6], grads[1]], targets, strict=True)
    copies = [pltpu.make_async_copy(*pair, copied.at[i]) for i, pair in enumerate(pairs)]
    for copy in copies:
        copy.start()
    rate_row[...] = jnp.zeros_like(rate_row)
    copies[0].wait()
    rate_row[:, :modes] = few[...]
    rates = rate_row[...]
    for shift in (modes, 2 * modes):
        rates = rates + pltpu.roll(rates, shift, 1)
    start = 0
    decays = []
    for at, length in enumerate((2 * block_len, seq_len - block_len, block_len)):
        delays = row_delays(block_len, seq_len, lax.broadcasted_iota(jnp.int32, (length, LANES), 0))
        decays.append(jnp.exp(delays[at](delays[3]).astype(F32) * (-1.0 / seq_len) * rates))
    copies[1].wait()
    for decay in decays:
        rows = pl.ds(start, decay.shape[0])
        table_ref[rows, :] = decay * wave[rows, :]
        start += decay.shape[0]
    for copy in copies[2:]:
        copy.wait()


def tables_kernel(modes, block_len, table_ref, fwd_ref, fwd_out, far_ref, here_ref, near_ref, spec_ref):
    period = 2 * block_len
    used = 4 * modes
    near_hi, near_lo = halves(table_ref[:period, :])
    fwd_hi, fwd_lo = halves(fwd_ref[...])
    spec = dot(fwd_hi, near_hi) + dot(fwd_hi, near_lo) + dot(fwd_lo, near_hi)
    fwd_out[:period, :] = fwd_hi[:, :block_len]
    fwd_out[period:, :] = fwd_lo[:, :block_len]
    spec_ref[...] = spec
    body = table_ref.shape[0] - block_len
    far_ref[...] = jnp.concatenate(halves(table_ref[period:body, :].T[:used]), axis=0)
    here_ref[...] = jnp.concatenate(halves(table_ref[body:, :].T[:used]), axis=0)
    place = lax.broadcasted_iota(jnp.int32, (period, LANES), 0)
    weight = jnp.where(lax.rem(place, block_len) == 0, 1.0 / period, 2.0 / period)
    spec_t = (spec * weight).T
    grad_rows = jnp.concatenate([spec_t[:modes], spec_t[2 * modes : 3 * modes]], axis=0)
    near_ref[...] = jnp.concatenate(halves(grad_rows), axis=0)


def main_kernel(modes, blocks, block_len, taps, channels, table_ref, short_ref, res_ref, fwd_ref, far_ref, here_ref,
                near_ref, grad_ref, mate_ref, *refs):
    bits = blocks.bit_length() - 1
    ids_refs, refs = refs[: bits + 1], refs[bits + 1 :]
    part_ref, query_ref, gated_ref, spec_ref, state_ref, onehot, ids = refs
    half = channels // 2
    groups = half // GROUP
    first = half_index() * half
    filled = 0
    for ref in ids_refs:
        ids[filled : filled + ref.shape[0], :] = ref[...]
        filled += ref.shape[0]
    seq_len = blocks * block_len
    vocab = table_ref.shape[1]
    own = lax.axis_index("ctx")
    order_one = order_matrix(block_len)
    order = jnp.concatenate([order_one * 16, order_one], axis=1)
    on_hi = (own & 1) == 1
    lane = lax.broadcasted_iota(jnp.int32, (block_len, LANES), 1).astype(F32)
    for place in range(blocks):
        source = lax.rem((own & -2) + 2 + place, blocks)
        flags = [((source ^ own) >> bit) & 1 for bit in range(bits)]
        slot = sum(flag << (bits - 1 - bit) for bit, flag in enumerate(flags) if bit > 0)
        slot = slot | (functools.reduce(lambda a, b: a ^ b, flags) << (bits - 1))
        row = ids[pl.ds(slot, 1), :]
        digits = jnp.concatenate([row >> 4, row & 15], axis=1).astype(F32)
        digits = jnp.broadcast_to(digits, (LANES, 2 * block_len)).astype(BF16)
        column = lax.dot_general(order, digits, (((1,), (1,)), ((), ())), preferred_element_type=F32)
        for piece in range(vocab // LANES):
            onehot[pl.ds(place * block_len, block_len), pl.ds(piece * LANES, LANES)] = jnp.where(
                column == lane + float(piece * LANES), 1.0, 0.0
            ).astype(BF16)
    body = seq_len - block_len
    period = 2 * block_len
    halo = SUBLANES * (taps - 1)
    rate = jnp.zeros((modes, 1), F32)
    last = lax.broadcasted_iota(jnp.int32, (halo, GROUP), 0) % SUBLANES == SUBLANES - 1

    def gather(group, part, rows):
        block = table_ref[pl.ds(pl.multiple_of(first + part * channels + group * GROUP, GROUP), GROUP), :]
        return lax.dot_general(onehot[rows:, :], block, (((1,), (1,)), ((), ())), preferred_element_type=F32)

    def features(group):
        return gather(group, 0, body - block_len - halo), gather(group, 1, 0), gather(group, 2, 0)

    def short_conv(feat, at, weights):
        tail = feat[(at - halo) % feat.shape[0] :][:halo]
        block = feat[at : at + block_len]
        ahead = jnp.where(last, tail, block[block_len - halo :]).reshape(taps - 1, SUBLANES, GROUP)
        ahead = pltpu.roll(ahead, 1, 1).reshape(halo, GROUP)
        padded = jnp.concatenate([ahead, block], axis=0)
        total = None
        for tap in range(taps):
            term = weights[tap : tap + 1] * padded[tap * SUBLANES : tap * SUBLANES + block_len]
            total = term if total is None else total + term
        return total

    def one_group(group, feats, rate):
        weights = [
            short_ref[:, pl.ds(pl.multiple_of(first + part * channels + group * GROUP, GROUP), GROUP)]
            for part in range(3)
        ]
        query = [short_conv(feats[0], halo + at, weights[0]) for at in (0, block_len)]
        query = jnp.concatenate(query, axis=1)
        gated = []
        for place in range(blocks):
            keys, vals = (short_conv(feats[part], place * block_len, weights[part]) for part in (1, 2))
            gated.append((keys * vals).astype(BF16))
        ahead_lo = jnp.concatenate([gated[-1], *gated[:-2]], axis=0)
        gated_far = jnp.concatenate([ahead_lo, jnp.concatenate(gated[:-1], axis=0)], axis=1)
        gated_own = jnp.concatenate(gated[-2:], axis=1)
        span = pl.ds(group * WIDE, WIDE)
        query_ref[:, span] = query
        gated_ref[:, span] = gated_own
        rows = pl.ds(group * GROUP, GROUP)
        own_grad, mate_grad = grad_ref[rows, :], mate_ref[rows, :]
        grads = jnp.concatenate(
            [jnp.where(on_hi, mate_grad, own_grad), jnp.where(on_hi, own_grad, mate_grad)], axis=0
        )
        grads = lax.dot_general(order_one, grads, (((1,), (1,)), ((), ())), preferred_element_type=F32)
        dconv = query * grads
        dconv_both = jnp.concatenate(halves(dconv), axis=0)
        spec = dot(fwd_ref[...], gated_own)
        spec = spec[:period] + spec[period:]
        spec_ref[:, span] = spec
        left = jnp.concatenate([fwd_ref[...], here_ref[...]], axis=0)
        dspec = dot(jnp.concatenate([left, left], axis=1), dconv_both)
        dstate = dspec[2 * period :]
        dspec = dspec[:period] + dspec[period : 2 * period]
        dstate = dstate[: 4 * modes] + dstate[4 * modes :]
        state = dot(far_ref[...], gated_far)
        state = state[: 4 * modes] + state[4 * modes :]
        left_re, left_im = spec[:block_len], spec[block_len:]
        right_re, right_im = dspec[:block_len], dspec[block_len:]
        leading = lax.broadcasted_iota(jnp.int32, (block_len, WIDE), 0) == 0
        rere, imim = left_re * right_re, left_im * right_im
        cross_re = jnp.where(leading, rere, rere + imim)
        cross_im = jnp.where(leading, imim, left_re * right_im - left_im * right_re)
        cross = jnp.concatenate([cross_re, cross_im], axis=0)
        cross_hi, cross_lo = halves(cross)
        near = near_ref[...]
        terms = dot(near, cross_hi) + dot(near, cross_lo)
        terms = terms[: 2 * modes] + terms[2 * modes :]
        sc, ss, sc1, ss1 = (state[i * modes : (i + 1) * modes] for i in range(4))
        dc, ds, dc1, ds1 = (dstate[i * modes : (i + 1) * modes] for i in range(4))
        grad = terms[:modes] + dc * sc - ds * ss
        slope = terms[modes:] + dc1 * sc + dc * sc1 - ds1 * ss - ds * ss1
        res = res_ref[:, pl.ds(pl.multiple_of(first + group * GROUP, GROUP), GROUP)]
        both = jnp.concatenate([res, res], axis=1)
        state_ref[:modes, span] = both * sc
        state_ref[modes:, span] = -(both * ss)
        grad = grad[:, :GROUP] + grad[:, GROUP:]
        slope = slope[:, :GROUP] + slope[:, GROUP:]
        for side in range(GROUP // LANES):
            at = (group * GROUP + side * LANES) // LANES * modes
            part_ref[pl.ds(at, modes), :] = grad[:, side * LANES : (side + 1) * LANES].astype(BF16)
        return rate + jnp.sum(res * slope, axis=1, keepdims=True)

    feats = features(0)
    for group in range(groups):
        ahead = features(group + 1) if group + 1 < groups else None
        rate = one_group(group, feats, rate)
        feats = ahead
    wide = jnp.broadcast_to(rate, (modes, LANES))
    square = jnp.concatenate([wide, jnp.zeros((LANES - modes, LANES), F32)], axis=0).T
    upper, lower = halves(jnp.broadcast_to(square[:1], (2 * SUBLANES, LANES)))
    row = lax.broadcasted_iota(jnp.int32, (2 * SUBLANES, LANES), 0)
    tail = jnp.where(row == 0, upper.astype(F32), jnp.where(row == 1, lower.astype(F32), 0.0))
    part_ref[pl.ds(half // LANES * modes, 2 * SUBLANES), :] = tail.astype(BF16)


def filter_kernel(modes, block_len, spec_ref, table_ref, res_ref, inv_ref, skip_ref, filt_ref, inv_out, skip_out, inv, copied):
    copies = [
        pltpu.make_async_copy(inv_ref, inv, copied.at[0]),
        pltpu.make_async_copy(skip_ref, skip_out, copied.at[1]),
    ]
    for copy in copies:
        copy.start()
    period = 2 * block_len
    spec_hi, spec_lo = halves(spec_ref[:, :modes])
    half = res_ref.shape[1] // 2
    res_hi, res_lo = halves(res_ref[:, pl.ds(pl.multiple_of(half_index() * half, half), half)])
    left = jnp.concatenate([spec_hi, spec_hi, spec_lo], axis=1)
    filt_ref[...] = dot(left, jnp.concatenate([res_hi, res_lo, res_hi], axis=0))
    for copy in copies:
        copy.wait()
    here = table_ref[table_ref.shape[0] - block_len :, : 2 * modes]
    inv_hi, inv_lo = halves(jnp.concatenate([inv[...], here], axis=1))
    inv_out[...] = jnp.concatenate([inv_hi, inv_lo], axis=0)


def mixed_kernel(block_len, query_ref, gated_ref, spec_ref, filt_ref, state_ref, inv_ref, skip_ref, own_ref, mate_ref):
    half = filt_ref.shape[1]
    first = half_index() * half
    on_hi = (lax.axis_index("ctx") & 1) == 1
    leading = lax.broadcasted_iota(jnp.int32, (block_len, WIDE), 0) == 0
    order = order_matrix(block_len, True)
    inv = inv_ref[...]
    for group in range(half // GROUP):
        span = pl.ds(group * WIDE, WIDE)
        rows = pl.ds(group * GROUP, GROUP)
        filt = filt_ref[:, rows]
        filt = jnp.concatenate([filt, filt], axis=1)
        skip = skip_ref[:, pl.ds(pl.multiple_of(first + group * GROUP, GROUP), GROUP)]
        left_re, left_im = filt[:block_len], filt[block_len:]
        right_re, right_im = spec_ref[:block_len, span], spec_ref[block_len:, span]
        rere, imim = left_re * right_re, left_im * right_im
        out_re = jnp.where(leading, rere, rere - imim)
        out_im = jnp.where(leading, imim, left_re * right_im + left_im * right_re)
        spec_hi, spec_lo = halves(jnp.concatenate([out_re, out_im, state_ref[:, span]], axis=0))
        conv = dot(inv, spec_hi)
        conv = conv[:block_len] + conv[block_len:] + dot(inv[:block_len], spec_lo)
        through = jnp.concatenate([skip, skip], axis=1) * gated_ref[:, span].astype(F32)
        mixed = dot(order, (query_ref[:, span] * (conv + through)).astype(BF16))
        low, high = mixed[:, :GROUP], mixed[:, GROUP:]
        own_ref[rows, :] = jnp.where(on_hi, high, low).T.astype(BF16)
        mate_ref[rows, :] = jnp.where(on_hi, low, high).T.astype(BF16)


def call(kernel, outs, scratch, args, cost, spaces=None, out_spaces=None):
    return pl.pallas_call(
        kernel,
        out_shape=[jax.ShapeDtypeStruct(shape, dtype) for shape, dtype in outs],
        in_specs=[pl.BlockSpec(memory_space=space) for space in spaces or [pltpu.VMEM] * len(args)],
        out_specs=[pl.BlockSpec(memory_space=space) for space in out_spaces or [pltpu.VMEM] * len(outs)],
        scratch_shapes=scratch,
        compiler_params=pltpu.CompilerParams(vmem_limit_bytes=40 * 1024 * 1024),
        cost_estimate=pl.CostEstimate(flops=cost[0], bytes_accessed=cost[1], transcendentals=0),
    )(*args)


def output_kernel(own_ref, mate_ref, mixed_ref, copied):
    half = own_ref.shape[0]
    second = half_index()
    copies = []
    for at, (source, place) in enumerate(((own_ref, second), (mate_ref, 1 - second))):
        target = mixed_ref.at[pl.ds(pl.multiple_of(place * half, half), half)]
        copies.append(pltpu.make_async_copy(source, target, copied.at[at]))
    for copy in copies:
        copy.start()
    for copy in copies:
        copy.wait()


def result_kernel(modes, part_ref, moved_ref, grad_ref, rate_ref):
    half = grad_ref.shape[1] // 2
    second = half_index()
    for tile in range(half // LANES):
        rows = pl.ds(tile * modes, modes)
        part, moved = part_ref[rows, :], moved_ref[rows, :]
        grad_ref[:, pl.ds(tile * LANES, LANES)] = jnp.where(second == 1, moved, part)
        grad_ref[:, pl.ds(half + tile * LANES, LANES)] = jnp.where(second == 1, part, moved)
    last = half // LANES * modes
    rate_ref[...] = (part_ref[last : last + 1, :] + moved_ref[last : last + 1, :])[:, :modes]


def rounded(value):
    return lax.reduce_precision(value, 8, 7)


def per_device(token_ids, feature_table, short_weight, residue, rates, skip_gain, grad_out):
    block_len = token_ids.shape[1]
    blocks = lax.axis_size("ctx")
    seq_len = block_len * blocks
    channels, modes = residue.shape
    taps = short_weight.shape[1]
    vocab = feature_table.shape[1]
    period = 2 * block_len
    forward, inverse = dft_tables(block_len)
    wave = mode_constants(block_len, seq_len, modes)
    half = channels // 2

    masks = [mask | 1 for mask in masks_of(blocks)[:0:-1]] + [1]
    moved_ids = [xor_permute(token_ids, ("ctx",), masks[0])]

    def in_hbm(*arrays):
        return [pltpu.with_memory_space_constraint(array, pltpu.HBM) for array in arrays]

    vmem, hbm = pltpu.VMEM, pltpu.HBM
    ids, short, res, forward, table, keep_grad, send_grad = call(
        functools.partial(inputs_kernel, modes, block_len, seq_len),
        [
            ((1, block_len), jnp.int32),
            (short_weight.shape[::-1], F32),
            ((modes, channels), F32),
            (forward.shape, F32),
            (wave.shape, F32),
            ((half, block_len), BF16),
            ((half, block_len), BF16),
        ],
        [
            vmem((1, modes), F32),
            vmem((1, LANES), F32),
            vmem(wave.shape, F32),
            pltpu.SemaphoreType.DMA((8,)),
        ],
        in_hbm(
            rates[None],
            jnp.asarray(wave),
            jnp.asarray(forward.astype(np.float32)),
            token_ids,
            residue.T,
            short_weight.T,
            grad_out[0],
        ),
        (10_000_000_000, 40_000_000),
        [hbm] * 7,
    )
    mate_grad = xor_permute(send_grad, ("ctx",), 1)
    for mask in masks[1:]:
        known = jnp.concatenate([ids, *moved_ids], axis=0)
        if mask == masks[-1]:
            known, table = lax.optimization_barrier((known, table))
        moved_ids.append(xor_permute(known, ("ctx",), mask))
    fwd, far, here, near, table_spec = call(
        functools.partial(tables_kernel, modes, block_len),
        [
            ((2 * period, block_len), BF16),
            ((8 * modes, seq_len - block_len), BF16),
            ((8 * modes, block_len), BF16),
            ((4 * modes, period), BF16),
            ((period, LANES), F32),
        ],
        [],
        [table, forward],
        (300_000_000, 1_000_000),
    )
    part, query, gated, spec, state = call(
        functools.partial(main_kernel, modes, blocks, block_len, taps, channels),
        [
            ((half // LANES * modes + 2 * SUBLANES, LANES), BF16),
            ((block_len, channels), F32),
            ((block_len, channels), BF16),
            ((period, channels), F32),
            ((2 * modes, channels), F32),
        ],
        [
            vmem((seq_len, vocab), BF16),
            vmem((blocks, block_len), jnp.int32),
        ],
        [feature_table, short, res, fwd, far, here, near, keep_grad, mate_grad, ids, *moved_ids],
        (4 * seq_len * vocab * channels, 6_000_000),
    )
    core = lax.axis_size("dp")
    hops = [mask | core for mask in masks_of(blocks * core) if mask != core]
    rows = half // LANES * modes
    sent = part
    filler = jnp.zeros((14, LANES), BF16)
    for hop in hops:
        if hop == hops[0]:
            sent, res = lax.optimization_barrier((sent, res))
            filt, inv, skip = call(
                functools.partial(filter_kernel, modes, block_len),
                [((period, half), F32), ((2 * block_len, period + 2 * modes), BF16), ((1, channels), F32)],
                [vmem(inverse.shape, F32), pltpu.SemaphoreType.DMA((2,))],
                [table_spec, table, res, *in_hbm(jnp.asarray(inverse.astype(np.float32)), skip_gain[None])],
                (50_000_000, 1_500_000),
                [vmem, vmem, vmem, hbm, hbm],
            )
        if hop == hops[1]:
            part, query, filt = lax.optimization_barrier((part, query, filt))
            mixed_own, mixed_mate = call(
                functools.partial(mixed_kernel, block_len),
                [((half, block_len), BF16)] * 2,
                [],
                [query, gated, spec, filt, state, inv, skip],
                (300_000_000, 3_000_000),
            )
        if hop == hops[2]:
            part, mixed_mate = lax.optimization_barrier((part, mixed_mate))
            mixed_moved = xor_permute(mixed_mate, ("ctx", "dp"), core)
        if hop == hops[3]:
            part, mixed_moved = lax.optimization_barrier((part, mixed_moved))
            (mixed,) = call(
                output_kernel,
                [((channels, block_len), BF16)],
                [pltpu.SemaphoreType.DMA((2,))],
                [mixed_own, mixed_moved],
                (0, 800_000),
                out_spaces=[hbm],
            )
        if hop == hops[0]:
            part, upper, lower = (sent[at].astype(F32) for at in (slice(rows), slice(rows, rows + 1), slice(rows + 1, rows + 2)))
        else:
            part, upper = rounded(part), rounded(rate)
            lower = rounded(rate - upper)
            sent = jnp.concatenate([part.astype(BF16), upper.astype(BF16), lower.astype(BF16), filler], axis=0)
        moved = xor_permute(sent, ("ctx", "dp"), hop).astype(F32)
        part = part + moved[:rows]
        rate = upper + lower + (moved[rows : rows + 1] + moved[rows + 1 : rows + 2])
    part = jnp.concatenate([part, rate, jnp.zeros((SUBLANES - 1, LANES), F32)], axis=0)
    part, mixed = lax.optimization_barrier((part, mixed))
    grad, rate = call(
        functools.partial(result_kernel, modes),
        [((modes, channels), F32), ((1, modes), F32)],
        [],
        [part, xor_permute(part, ("ctx", "dp"), core)],
        (0, 200_000),
    )
    return (mixed[None], grad.T, rate[0])


def solution(mesh):
    return jax.shard_map(
        per_device,
        mesh=mesh,
        in_specs=(P("dp", "ctx"), P(), P(), P(), P(), P(), P("dp", None, "ctx")),
        out_specs=(P("dp", None, "ctx"), P(), P()),
        check_vma=False,
    )
```

```python
import functools
import math

import jax
import jax.numpy as jnp
import numpy as np
from jax import lax
from jax.experimental import pallas as pl
from jax.experimental.pallas import tpu as pltpu
from jax.sharding import PartitionSpec as P

F32 = jnp.float32
BF16 = jnp.bfloat16
GROUP = 256
WIDE = 2 * GROUP
SUBLANES = 8
LANES = 128


def xor_permute(block, axis, mask):
    size = math.prod(lax.axis_size(name) for name in axis)
    return lax.ppermute(block, axis, [(i, i ^ mask) for i in range(size)])


def masks_of(size):
    return [1 << bit for bit in range(size.bit_length() - 1)]


def half_index():
    bits = lax.axis_index("ctx") ^ lax.axis_index("dp")
    for shift in (4, 2, 1):
        bits = bits ^ (bits >> shift)
    return bits & 1


def halves(table):
    upper = table.astype(BF16)
    return upper, (table - upper.astype(F32)).astype(BF16)


def dot(left, right):
    return jnp.dot(left, right, preferred_element_type=F32)


def row_token(row, block_len):
    return row % SUBLANES * (block_len // SUBLANES) + row // SUBLANES


def order_matrix(block_len, transposed=False):
    row = lax.broadcasted_iota(jnp.int32, (block_len, block_len), 1 if transposed else 0)
    token = lax.broadcasted_iota(jnp.int32, (block_len, block_len), 0 if transposed else 1)
    return jnp.where(row_token(row, block_len) == token, 1.0, 0.0).astype(BF16)


def dft_tables(block_len):
    period = 2 * block_len
    column = np.arange(block_len)[:, None]
    row = np.arange(block_len)
    sample = np.concatenate([row_token(row, block_len), block_len + row_token(row, block_len)])[None, :]
    angle = (column * sample % period) * (2.0 * math.pi / period)
    parity = 1.0 - 2.0 * (sample % 2)
    imag = np.where(column == 0, parity, -np.sin(angle))
    forward = np.concatenate([np.cos(angle), imag], axis=0)
    weight = np.where(np.arange(period) % block_len == 0, 1.0, 2.0) / period
    inverse = (forward[:, :block_len] * weight[:, None]).T
    return forward, inverse


def row_delays(block_len, seq_len, row):
    token = row_token(row % block_len, block_len) + row // block_len * block_len
    period = 2 * block_len
    body = seq_len - block_len

    def near(n):
        return n + (n >= block_len) * (seq_len - period)

    return near, lambda n: body - n, lambda n: n, token


def mode_constants(block_len, seq_len, modes):
    parts = []
    for at, length in enumerate((2 * block_len, seq_len - block_len, block_len)):
        delays = row_delays(block_len, seq_len, np.arange(length))
        parts.append(delays[at](delays[3]))
    delay = np.concatenate(parts)[:, None]
    period = 2 * modes + 2
    angle = (delay * (np.arange(modes)[None, :] + 1) % period) * (2.0 * math.pi / period)
    ratio = delay / seq_len
    parts = [np.cos(angle), np.sin(angle), -ratio * np.cos(angle), -ratio * np.sin(angle)]
    wave = np.concatenate(parts, axis=1)
    return np.pad(wave, ((0, 0), (0, LANES - wave.shape[1]))).astype(np.float32)


def inputs_kernel(modes, block_len, seq_len, *refs):
    sources, outs, scratch = refs[:7], refs[7:14], refs[14:]
    ids_out, short_out, res_out, fwd_out, table_ref, keep_ref, send_ref = outs
    few, rate_row, wave, copied = scratch
    half = keep_ref.shape[0]
    second = half_index()
    grads = [sources[6].at[pl.ds(pl.multiple_of(place * half, half), half)] for place in (1 - second, second)]
    targets = [few, wave, send_ref, fwd_out, ids_out, res_out, short_out, keep_ref]
    pairs = zip([*sources[:2], grads[0], *sources[2:6], grads[1]], targets, strict=True)
    copies = [pltpu.make_async_copy(*pair, copied.at[i]) for i, pair in enumerate(pairs)]
    for copy in copies:
        copy.start()
    rate_row[...] = jnp.zeros_like(rate_row)
    copies[0].wait()
    rate_row[:, :modes] = few[...]
    rates = rate_row[...]
    for shift in (modes, 2 * modes):
        rates = rates + pltpu.roll(rates, shift, 1)
    start = 0
    decays = []
    for at, length in enumerate((2 * block_len, seq_len - block_len, block_len)):
        delays = row_delays(block_len, seq_len, lax.broadcasted_iota(jnp.int32, (length, LANES), 0))
        decays.append(jnp.exp(delays[at](delays[3]).astype(F32) * (-1.0 / seq_len) * rates))
    copies[1].wait()
    for decay in decays:
        rows = pl.ds(start, decay.shape[0])
        table_ref[rows, :] = decay * wave[rows, :]
        start += decay.shape[0]
    for copy in copies[2:]:
        copy.wait()


def tables_kernel(modes, block_len, table_ref, fwd_ref, fwd_out, far_ref, here_ref, near_ref, spec_ref):
    period = 2 * block_len
    used = 4 * modes
    near_hi, near_lo = halves(table_ref[:period, :])
    fwd_hi, fwd_lo = halves(fwd_ref[...])
    spec = dot(fwd_hi, near_hi) + dot(fwd_hi, near_lo) + dot(fwd_lo, near_hi)
    fwd_out[:period, :] = fwd_hi[:, :block_len]
    fwd_out[period:, :] = fwd_lo[:, :block_len]
    spec_ref[...] = spec
    body = table_ref.shape[0] - block_len
    far_ref[...] = jnp.concatenate(halves(table_ref[period:body, :].T[:used]), axis=0)
    here_ref[...] = jnp.concatenate(halves(table_ref[body:, :].T[:used]), axis=0)
    place = lax.broadcasted_iota(jnp.int32, (period, LANES), 0)
    weight = jnp.where(lax.rem(place, block_len) == 0, 1.0 / period, 2.0 / period)
    spec_t = (spec * weight).T
    grad_rows = jnp.concatenate([spec_t[:modes], spec_t[2 * modes : 3 * modes]], axis=0)
    near_ref[...] = jnp.concatenate(halves(grad_rows), axis=0)


def main_kernel(modes, blocks, block_len, taps, channels, table_ref, short_ref, res_ref, fwd_ref, far_ref, here_ref,
                near_ref, grad_ref, mate_ref, *refs):
    bits = blocks.bit_length() - 1
    ids_refs, refs = refs[: bits + 1], refs[bits + 1 :]
    part_ref, query_ref, gated_ref, spec_ref, state_ref, onehot, ids = refs
    half = channels // 2
    groups = half // GROUP
    first = half_index() * half
    filled = 0
    for ref in ids_refs:
        ids[filled : filled + ref.shape[0], :] = ref[...]
        filled += ref.shape[0]
    seq_len = blocks * block_len
    vocab = table_ref.shape[1]
    own = lax.axis_index("ctx")
    order_one = order_matrix(block_len)
    order = jnp.concatenate([order_one * 16, order_one], axis=1)
    on_hi = (own & 1) == 1
    lane = lax.broadcasted_iota(jnp.int32, (block_len, LANES), 1).astype(F32)
    for place in range(blocks):
        source = lax.rem((own & -2) + 2 + place, blocks)
        flags = [((source ^ own) >> bit) & 1 for bit in range(bits)]
        slot = sum(flag << (bits - 1 - bit) for bit, flag in enumerate(flags) if bit > 0)
        slot = slot | (functools.reduce(lambda a, b: a ^ b, flags) << (bits - 1))
        row = ids[pl.ds(slot, 1), :]
        digits = jnp.concatenate([row >> 4, row & 15], axis=1).astype(F32)
        digits = jnp.broadcast_to(digits, (LANES, 2 * block_len)).astype(BF16)
        column = lax.dot_general(order, digits, (((1,), (1,)), ((), ())), preferred_element_type=F32)
        for piece in range(vocab // LANES):
            onehot[pl.ds(place * block_len, block_len), pl.ds(piece * LANES, LANES)] = jnp.where(
                column == lane + float(piece * LANES), 1.0, 0.0
            ).astype(BF16)
    body = seq_len - block_len
    period = 2 * block_len
    halo = SUBLANES * (taps - 1)
    rate = jnp.zeros((modes, 1), F32)
    last = lax.broadcasted_iota(jnp.int32, (halo, GROUP), 0) % SUBLANES == SUBLANES - 1

    def gather(group, part, rows):
        block = table_ref[pl.ds(pl.multiple_of(first + part * channels + group * GROUP, GROUP), GROUP), :]
        return lax.dot_general(onehot[rows:, :], block, (((1,), (1,)), ((), ())), preferred_element_type=F32)

    def features(group):
        return gather(group, 0, body - block_len - halo), gather(group, 1, 0), gather(group, 2, 0)

    def short_conv(feat, at, weights):
        tail = feat[(at - halo) % feat.shape[0] :][:halo]
        block = feat[at : at + block_len]
        ahead = jnp.where(last, tail, block[block_len - halo :]).reshape(taps - 1, SUBLANES, GROUP)
        ahead = pltpu.roll(ahead, 1, 1).reshape(halo, GROUP)
        padded = jnp.concatenate([ahead, block], axis=0)
        total = None
        for tap in range(taps):
            term = weights[tap : tap + 1] * padded[tap * SUBLANES : tap * SUBLANES + block_len]
            total = term if total is None else total + term
        return total

    def one_group(group, feats, rate):
        weights = [
            short_ref[:, pl.ds(pl.multiple_of(first + part * channels + group * GROUP, GROUP), GROUP)]
            for part in range(3)
        ]
        query = [short_conv(feats[0], halo + at, weights[0]) for at in (0, block_len)]
        query = jnp.concatenate(query, axis=1)
        gated = []
        for place in range(blocks):
            keys, vals = (short_conv(feats[part], place * block_len, weights[part]) for part in (1, 2))
            gated.append((keys * vals).astype(BF16))
        ahead_lo = jnp.concatenate([gated[-1], *gated[:-2]], axis=0)
        gated_far = jnp.concatenate([ahead_lo, jnp.concatenate(gated[:-1], axis=0)], axis=1)
        gated_own = jnp.concatenate(gated[-2:], axis=1)
        span = pl.ds(group * WIDE, WIDE)
        query_ref[:, span] = query
        gated_ref[:, span] = gated_own
        rows = pl.ds(group * GROUP, GROUP)
        own_grad, mate_grad = grad_ref[rows, :], mate_ref[rows, :]
        grads = jnp.concatenate(
            [jnp.where(on_hi, mate_grad, own_grad), jnp.where(on_hi, own_grad, mate_grad)], axis=0
        )
        grads = lax.dot_general(order_one, grads, (((1,), (1,)), ((), ())), preferred_element_type=F32)
        dconv = query * grads
        dconv_both = jnp.concatenate(halves(dconv), axis=0)
        spec = dot(fwd_ref[...], gated_own)
        spec = spec[:period] + spec[period:]
        spec_ref[:, span] = spec
        left = jnp.concatenate([fwd_ref[...], here_ref[...]], axis=0)
        dspec = dot(jnp.concatenate([left, left], axis=1), dconv_both)
        dstate = dspec[2 * period :]
        dspec = dspec[:period] + dspec[period : 2 * period]
        dstate = dstate[: 4 * modes] + dstate[4 * modes :]
        state = dot(far_ref[...], gated_far)
        state = state[: 4 * modes] + state[4 * modes :]
        left_re, left_im = spec[:block_len], spec[block_len:]
        right_re, right_im = dspec[:block_len], dspec[block_len:]
        leading = lax.broadcasted_iota(jnp.int32, (block_len, WIDE), 0) == 0
        rere, imim = left_re * right_re, left_im * right_im
        cross_re = jnp.where(leading, rere, rere + imim)
        cross_im = jnp.where(leading, imim, left_re * right_im - left_im * right_re)
        cross = jnp.concatenate([cross_re, cross_im], axis=0)
        cross_hi = cross.astype(BF16)
        near = near_ref[...]
        terms = dot(near, cross_hi)
        terms = terms[: 2 * modes] + terms[2 * modes :]
        sc, ss, sc1, ss1 = (state[i * modes : (i + 1) * modes] for i in range(4))
        dc, ds, dc1, ds1 = (dstate[i * modes : (i + 1) * modes] for i in range(4))
        grad = terms[:modes] + dc * sc - ds * ss
        slope = terms[modes:] + dc1 * sc + dc * sc1 - ds1 * ss - ds * ss1
        res = res_ref[:, pl.ds(pl.multiple_of(first + group * GROUP, GROUP), GROUP)]
        both = jnp.concatenate([res, res], axis=1)
        state_ref[:modes, span] = both * sc
        state_ref[modes:, span] = -(both * ss)
        grad = grad[:, :GROUP] + grad[:, GROUP:]
        slope = slope[:, :GROUP] + slope[:, GROUP:]
        for side in range(GROUP // LANES):
            at = (group * GROUP + side * LANES) // LANES * modes
            part_ref[pl.ds(at, modes), :] = grad[:, side * LANES : (side + 1) * LANES].astype(BF16)
        return rate + jnp.sum(res * slope, axis=1, keepdims=True)

    feats = features(0)
    for group in range(groups):
        ahead = features(group + 1) if group + 1 < groups else None
        rate = one_group(group, feats, rate)
        feats = ahead
    wide = jnp.broadcast_to(rate, (modes, LANES))
    square = jnp.concatenate([wide, jnp.zeros((LANES - modes, LANES), F32)], axis=0).T
    upper, lower = halves(jnp.broadcast_to(square[:1], (2 * SUBLANES, LANES)))
    row = lax.broadcasted_iota(jnp.int32, (2 * SUBLANES, LANES), 0)
    tail = jnp.where(row == 0, upper.astype(F32), jnp.where(row == 1, lower.astype(F32), 0.0))
    part_ref[pl.ds(half // LANES * modes, 2 * SUBLANES), :] = tail.astype(BF16)


def filter_kernel(modes, block_len, spec_ref, table_ref, res_ref, inv_ref, skip_ref, filt_ref, inv_out, skip_out, inv, copied):
    copies = [
        pltpu.make_async_copy(inv_ref, inv, copied.at[0]),
        pltpu.make_async_copy(skip_ref, skip_out, copied.at[1]),
    ]
    for copy in copies:
        copy.start()
    period = 2 * block_len
    spec_hi, spec_lo = halves(spec_ref[:, :modes])
    half = res_ref.shape[1] // 2
    res_hi, res_lo = halves(res_ref[:, pl.ds(pl.multiple_of(half_index() * half, half), half)])
    left = jnp.concatenate([spec_hi, spec_hi, spec_lo], axis=1)
    filt_ref[...] = dot(left, jnp.concatenate([res_hi, res_lo, res_hi], axis=0))
    for copy in copies:
        copy.wait()
    here = table_ref[table_ref.shape[0] - block_len :, : 2 * modes]
    inv_hi, inv_lo = halves(jnp.concatenate([inv[...], here], axis=1))
    inv_out[...] = jnp.concatenate([inv_hi, inv_lo], axis=0)


def mixed_kernel(block_len, query_ref, gated_ref, spec_ref, filt_ref, state_ref, inv_ref, skip_ref, own_ref, mate_ref):
    half = filt_ref.shape[1]
    first = half_index() * half
    on_hi = (lax.axis_index("ctx") & 1) == 1
    leading = lax.broadcasted_iota(jnp.int32, (block_len, WIDE), 0) == 0
    order = order_matrix(block_len, True)
    inv = inv_ref[...]
    for group in range(half // GROUP):
        span = pl.ds(group * WIDE, WIDE)
        rows = pl.ds(group * GROUP, GROUP)
        filt = filt_ref[:, rows]
        filt = jnp.concatenate([filt, filt], axis=1)
        skip = skip_ref[:, pl.ds(pl.multiple_of(first + group * GROUP, GROUP), GROUP)]
        left_re, left_im = filt[:block_len], filt[block_len:]
        right_re, right_im = spec_ref[:block_len, span], spec_ref[block_len:, span]
        rere, imim = left_re * right_re, left_im * right_im
        out_re = jnp.where(leading, rere, rere - imim)
        out_im = jnp.where(leading, imim, left_re * right_im + left_im * right_re)
        spec_hi, spec_lo = halves(jnp.concatenate([out_re, out_im, state_ref[:, span]], axis=0))
        conv = dot(inv, spec_hi)
        conv = conv[:block_len] + conv[block_len:] + dot(inv[:block_len], spec_lo)
        through = jnp.concatenate([skip, skip], axis=1) * gated_ref[:, span].astype(F32)
        mixed = dot(order, (query_ref[:, span] * (conv + through)).astype(BF16))
        low, high = mixed[:, :GROUP], mixed[:, GROUP:]
        own_ref[rows, :] = jnp.where(on_hi, high, low).T.astype(BF16)
        mate_ref[rows, :] = jnp.where(on_hi, low, high).T.astype(BF16)


def call(kernel, outs, scratch, args, cost, spaces=None, out_spaces=None):
    return pl.pallas_call(
        kernel,
        out_shape=[jax.ShapeDtypeStruct(shape, dtype) for shape, dtype in outs],
        in_specs=[pl.BlockSpec(memory_space=space) for space in spaces or [pltpu.VMEM] * len(args)],
        out_specs=[pl.BlockSpec(memory_space=space) for space in out_spaces or [pltpu.VMEM] * len(outs)],
        scratch_shapes=scratch,
        compiler_params=pltpu.CompilerParams(vmem_limit_bytes=40 * 1024 * 1024),
        cost_estimate=pl.CostEstimate(flops=cost[0], bytes_accessed=cost[1], transcendentals=0),
    )(*args)


def output_kernel(own_ref, mate_ref, mixed_ref, copied):
    half = own_ref.shape[0]
    second = half_index()
    copies = []
    for at, (source, place) in enumerate(((own_ref, second), (mate_ref, 1 - second))):
        target = mixed_ref.at[pl.ds(pl.multiple_of(place * half, half), half)]
        copies.append(pltpu.make_async_copy(source, target, copied.at[at]))
    for copy in copies:
        copy.start()
    for copy in copies:
        copy.wait()


def result_kernel(modes, part_ref, moved_ref, grad_ref, rate_ref):
    half = grad_ref.shape[1] // 2
    second = half_index()
    for tile in range(half // LANES):
        rows = pl.ds(tile * modes, modes)
        part, moved = part_ref[rows, :], moved_ref[rows, :]
        grad_ref[:, pl.ds(tile * LANES, LANES)] = jnp.where(second == 1, moved, part)
        grad_ref[:, pl.ds(half + tile * LANES, LANES)] = jnp.where(second == 1, part, moved)
    last = half // LANES * modes
    rate_ref[...] = (part_ref[last : last + 1, :] + moved_ref[last : last + 1, :])[:, :modes]


def rounded(value):
    return lax.reduce_precision(value, 8, 7)


def per_device(token_ids, feature_table, short_weight, residue, rates, skip_gain, grad_out):
    block_len = token_ids.shape[1]
    blocks = lax.axis_size("ctx")
    seq_len = block_len * blocks
    channels, modes = residue.shape
    taps = short_weight.shape[1]
    vocab = feature_table.shape[1]
    period = 2 * block_len
    forward, inverse = dft_tables(block_len)
    wave = mode_constants(block_len, seq_len, modes)
    half = channels // 2

    masks = [mask | 1 for mask in masks_of(blocks)[:0:-1]] + [1]
    moved_ids = [xor_permute(token_ids, ("ctx",), masks[0])]

    def in_hbm(*arrays):
        return [pltpu.with_memory_space_constraint(array, pltpu.HBM) for array in arrays]

    vmem, hbm = pltpu.VMEM, pltpu.HBM
    ids, short, res, forward, table, keep_grad, send_grad = call(
        functools.partial(inputs_kernel, modes, block_len, seq_len),
        [
            ((1, block_len), jnp.int32),
            (short_weight.shape[::-1], F32),
            ((modes, channels), F32),
            (forward.shape, F32),
            (wave.shape, F32),
            ((half, block_len), BF16),
            ((half, block_len), BF16),
        ],
        [
            vmem((1, modes), F32),
            vmem((1, LANES), F32),
            vmem(wave.shape, F32),
            pltpu.SemaphoreType.DMA((8,)),
        ],
        in_hbm(
            rates[None],
            jnp.asarray(wave),
            jnp.asarray(forward.astype(np.float32)),
            token_ids,
            residue.T,
            short_weight.T,
            grad_out[0],
        ),
        (10_000_000_000, 40_000_000),
        [hbm] * 7,
    )
    mate_grad = xor_permute(send_grad, ("ctx",), 1)
    for mask in masks[1:]:
        known = jnp.concatenate([ids, *moved_ids], axis=0)
        if mask == masks[-1]:
            known, table = lax.optimization_barrier((known, table))
        moved_ids.append(xor_permute(known, ("ctx",), mask))
    fwd, far, here, near, table_spec = call(
        functools.partial(tables_kernel, modes, block_len),
        [
            ((2 * period, block_len), BF16),
            ((8 * modes, seq_len - block_len), BF16),
            ((8 * modes, block_len), BF16),
            ((4 * modes, period), BF16),
            ((period, LANES), F32),
        ],
        [],
        [table, forward],
        (300_000_000, 1_000_000),
    )
    part, query, gated, spec, state = call(
        functools.partial(main_kernel, modes, blocks, block_len, taps, channels),
        [
            ((half // LANES * modes + 2 * SUBLANES, LANES), BF16),
            ((block_len, channels), F32),
            ((block_len, channels), BF16),
            ((period, channels), F32),
            ((2 * modes, channels), F32),
        ],
        [
            vmem((seq_len, vocab), BF16),
            vmem((blocks, block_len), jnp.int32),
        ],
        [feature_table, short, res, fwd, far, here, near, keep_grad, mate_grad, ids, *moved_ids],
        (4 * seq_len * vocab * channels, 6_000_000),
    )
    core = lax.axis_size("dp")
    hops = [mask | core for mask in masks_of(blocks * core) if mask != core]
    rows = half // LANES * modes
    sent = part
    filler = jnp.zeros((14, LANES), BF16)
    for hop in hops:
        if hop == hops[0]:
            sent, res = lax.optimization_barrier((sent, res))
            filt, inv, skip = call(
                functools.partial(filter_kernel, modes, block_len),
                [((period, half), F32), ((2 * block_len, period + 2 * modes), BF16), ((1, channels), F32)],
                [vmem(inverse.shape, F32), pltpu.SemaphoreType.DMA((2,))],
                [table_spec, table, res, *in_hbm(jnp.asarray(inverse.astype(np.float32)), skip_gain[None])],
                (50_000_000, 1_500_000),
                [vmem, vmem, vmem, hbm, hbm],
            )
        if hop == hops[1]:
            part, query, filt = lax.optimization_barrier((part, query, filt))
            mixed_own, mixed_mate = call(
                functools.partial(mixed_kernel, block_len),
                [((half, block_len), BF16)] * 2,
                [],
                [query, gated, spec, filt, state, inv, skip],
                (300_000_000, 3_000_000),
            )
        if hop == hops[2]:
            part, mixed_mate = lax.optimization_barrier((part, mixed_mate))
            mixed_moved = xor_permute(mixed_mate, ("ctx", "dp"), core)
        if hop == hops[3]:
            part, mixed_moved = lax.optimization_barrier((part, mixed_moved))
            (mixed,) = call(
                output_kernel,
                [((channels, block_len), BF16)],
                [pltpu.SemaphoreType.DMA((2,))],
                [mixed_own, mixed_moved],
                (0, 800_000),
                out_spaces=[hbm],
            )
        if hop == hops[0]:
            part, upper, lower = (sent[at].astype(F32) for at in (slice(rows), slice(rows, rows + 1), slice(rows + 1, rows + 2)))
        else:
            part, upper = rounded(part), rounded(rate)
            lower = rounded(rate - upper)
            sent = jnp.concatenate([part.astype(BF16), upper.astype(BF16), lower.astype(BF16), filler], axis=0)
        moved = xor_permute(sent, ("ctx", "dp"), hop).astype(F32)
        part = part + moved[:rows]
        rate = upper + lower + (moved[rows : rows + 1] + moved[rows + 1 : rows + 2])
    part = jnp.concatenate([part, rate, jnp.zeros((SUBLANES - 1, LANES), F32)], axis=0)
    part, mixed = lax.optimization_barrier((part, mixed))
    grad, rate = call(
        functools.partial(result_kernel, modes),
        [((modes, channels), F32), ((1, modes), F32)],
        [],
        [part, xor_permute(part, ("ctx", "dp"), core)],
        (0, 200_000),
    )
    return (mixed[None], grad.T, rate[0])


def solution(mesh):
    return jax.shard_map(
        per_device,
        mesh=mesh,
        in_specs=(P("dp", "ctx"), P(), P(), P(), P(), P(), P("dp", None, "ctx")),
        out_specs=(P("dp", None, "ctx"), P(), P()),
        check_vma=False,
    )
```
